32 devices in a mesh: rep: 4 (over x, core), ctx: 8 (over z, y).
Axes of the slice: x: 2, y: 2, z: 4, core: 2. Of those that a mesh axis runs over, the one named last changes fastest.
Arguments:
- tokens: bfloat16 [8, 1024, 1536], P('rep', 'ctx'), may hold values from -6 to 6
- cotangent: bfloat16 [8, 1024, 1536], P('rep', 'ctx'), may hold values from -6 to 6
- query_weight: float32 [1536, 1536], P('ctx'), may hold values from -0.15625 to 0.15625
- key_weight: float32 [1536, 512], P('ctx'), may hold values from -0.15625 to 0.15625
- value_weight: float32 [1536, 512], P('ctx'), may hold values from -0.15625 to 0.15625
- output_weight: float32 [1536, 1536], P('ctx'), may hold values from -0.625 to 0.625
- gate_weight: float32 [1536, 6912], P('ctx'), may hold values from -0.15625 to 0.15625
- up_weight: float32 [1536, 6912], P('ctx'), may hold values from -0.15625 to 0.15625
- down_weight: float32 [6912, 1536], P('ctx'), may hold values from -0.078125 to 0.078125
- norm_gains: float32 [1600, 2], P('ctx'), may hold values from 0.5 to 1.5
- first_query: float32 [1536, 1536], P('ctx'), may hold values from -24 to 24
- first_key: float32 [1536, 512], P('ctx'), may hold values from -32 to 32
- first_value: float32 [1536, 512], P('ctx'), may hold values from -32 to 32
- first_output: float32 [1536, 1536], P('ctx'), may hold values from -6 to 6
- first_gate: float32 [1536, 6912], P('ctx'), may hold values from -32 to 32
- first_up: float32 [1536, 6912], P('ctx'), may hold values from -32 to 32
- first_down: float32 [6912, 1536], P('ctx'), may hold values from -32 to 32
- first_gains: float32 [1600, 2], P('ctx'), may hold values from -80 to 80
- second_query: float32 [1536, 1536], P('ctx'), may hold values from 69.632 to 278.528
- second_key: float32 [1536, 512], P('ctx'), may hold values from 106.496 to 425.984
- second_value: float32 [1536, 512], P('ctx'), may hold values from 155.648 to 622.592
- second_output: float32 [1536, 1536], P('ctx'), may hold values from 3.84 to 15.2
- second_gate: float32 [1536, 6912], P('ctx'), may hold values from 155.648 to 622.592
- second_up: float32 [1536, 6912], P('ctx'), may hold values from 155.648 to 622.592
- second_down: float32 [6912, 1536], P('ctx'), may hold values from 155.648 to 622.592
- second_gains: float32 [1600, 2], P('ctx'), may hold values from 737.28 to 2949.12
Outputs:
- activations: bfloat16 [8, 1024, 1536], P('rep', 'ctx')
- input_gradient: float32 [8, 1024, 1536], P('rep', 'ctx')
- query_new: float32 [1536, 1536], P('ctx')
- key_new: float32 [1536, 512], P('ctx')
- value_new: float32 [1536, 512], P('ctx')
- output_new: float32 [1536, 1536], P('ctx')
- gate_new: float32 [1536, 6912], P('ctx')
- up_new: float32 [1536, 6912], P('ctx')
- down_new: float32 [6912, 1536], P('ctx')
- gains_new: float32 [1600, 2], P('ctx')
- first_query_new: float32 [1536, 1536], P('ctx')
- first_key_new: float32 [1536, 512], P('ctx')
- first_value_new: float32 [1536, 512], P('ctx')
- first_output_new: float32 [1536, 1536], P('ctx')
- first_gate_new: float32 [1536, 6912], P('ctx')
- first_up_new: float32 [1536, 6912], P('ctx')
- first_down_new: float32 [6912, 1536], P('ctx')
- first_gains_new: float32 [1600, 2], P('ctx')
- second_query_new: float32 [1536, 1536], P('ctx')
- second_key_new: float32 [1536, 512], P('ctx')
- second_value_new: float32 [1536, 512], P('ctx')
- second_output_new: float32 [1536, 1536], P('ctx')
- second_gate_new: float32 [1536, 6912], P('ctx')
- second_up_new: float32 [1536, 6912], P('ctx')
- second_down_new: float32 [6912, 1536], P('ctx')
- second_gains_new: float32 [1600, 2], P('ctx')
The draws below stay inside these ranges and needn't reach their ends.
All inputs are finite; a program needn't handle non-finite values.
Results may differ from the reference program's by a relative error of at most 0.025.
Values may be sent and summed in bfloat16 or wider, within the bound.
A program may use at most 448 MiB of HBM per device.

```python
import math
import jax
import jax.numpy as jnp
from jax import lax

D = 1536
FF = 6912
H = 24
KV = 8
HD = 64
STEP = 5
SEQ = 1024
BATCH = 8
TOKENS = 8192


def block_levels(key, dims, shards, smallest, top_value):
    def one(axis_at, parts):
        draws = jax.random.uniform(jax.random.fold_in(jax.random.fold_in(key, 6), axis_at), (parts,), jnp.float32, smallest / len(shards), top_value / len(shards))
        return jnp.repeat(jnp.exp(draws), dims[axis_at] // parts).reshape((-1,) + (1,) * (len(dims) - axis_at - 1))

    gain = one(*shards[0])
    for cut in shards[1:]:
        gain = gain * one(*cut)
    return gain


def noise(rng, shape, deviation, reach, cuts=(), kind=jnp.bfloat16):
    values = jax.random.normal(rng, shape, jnp.float32) * deviation
    if len(cuts) > 0:
        values = block_levels(rng, shape, cuts, -0.22, 0.18) * values
    return jnp.clip(values, min=-reach, max=reach).astype(kind)


def setup_inputs(seed: int = 0) -> dict:
    key_list = jax.random.split(jax.random.key(seed), 27)
    tokens = noise(key_list[0], (BATCH, SEQ, D), 1.0, 6.0, ((0, 4), (1, 8)))
    cotangent = noise(key_list[1], (BATCH, SEQ, D), 1.0, 6.0, ((0, 4), (1, 8)))
    query_weight = noise(key_list[2], (D, H * HD), D ** -0.5, 0.15625, ((0, 8),), jnp.float32)
    key_weight = noise(key_list[3], (D, KV * HD), D ** -0.5, 0.15625, ((0, 8),), jnp.float32)
    value_weight = noise(key_list[4], (D, KV * HD), D ** -0.5, 0.15625, ((0, 8),), jnp.float32)
    output_weight = noise(key_list[5], (H * HD, D), (max(1, H * HD * 64 // SEQ)) ** -0.5, 0.625, ((0, 8),), jnp.float32)
    gate_weight = noise(key_list[6], (D, FF), D ** -0.5, 0.15625, ((0, 8),), jnp.float32)
    up_weight = noise(key_list[7], (D, FF), D ** -0.5, 0.15625, ((0, 8),), jnp.float32)
    down_weight = noise(key_list[8], (FF, D), FF ** -0.5, 0.078125, ((0, 8),), jnp.float32)
    norm_gains = jnp.clip(1.0 + 0.1 * jax.random.normal(key_list[9], (D + HD, 2), jnp.float32), 0.5, 1.5)
    first_query = noise(key_list[10], (D, H * HD), (0.044 * TOKENS ** 0.5), 24.0, ((0, 8),), jnp.float32)
    first_key = noise(key_list[11], (D, KV * HD), (0.055 * TOKENS ** 0.5), 32.0, ((0, 8),), jnp.float32)
    first_value = noise(key_list[12], (D, KV * HD), (0.066 * TOKENS ** 0.5), 32.0, ((0, 8),), jnp.float32)
    first_output = noise(key_list[13], (H * HD, D), (0.33 * BATCH ** 0.5), 6.0, ((0, 8),), jnp.float32)
    first_gate = noise(key_list[14], (D, FF), (0.066 * TOKENS ** 0.5), 32.0, ((0, 8),), jnp.float32)
    first_up = noise(key_list[15], (D, FF), (0.066 * TOKENS ** 0.5), 32.0, ((0, 8),), jnp.float32)
    first_down = noise(key_list[16], (FF, D), (0.066 * TOKENS ** 0.5), 32.0, ((0, 8),), jnp.float32)
    first_gains = noise(key_list[17], (D + HD, 2), (0.14 * TOKENS ** 0.5), 80.0, ((0, 8),), jnp.float32)
    second_query = jnp.clip(jnp.exp(math.log(278.528) - 1.3862944 * jax.random.uniform(key_list[18], (D, H * HD), jnp.float32) ** block_levels(key_list[18], (D, H * HD), ((0, 8),), -0.2, 0.2)), 69.632, 278.528)
    second_key = jnp.clip(jnp.exp(math.log(425.984) - 1.3862944 * jax.random.uniform(key_list[19], (D, KV * HD), jnp.float32) ** block_levels(key_list[19], (D, KV * HD), ((0, 8),), -0.2, 0.2)), 106.496, 425.984)
    second_value = jnp.clip(jnp.exp(math.log(622.592) - 1.3862944 * jax.random.uniform(key_list[20], (D, KV * HD), jnp.float32) ** block_levels(key_list[20], (D, KV * HD), ((0, 8),), -0.2, 0.2)), 155.648, 622.592)
    second_output = jnp.clip(jnp.exp(math.log(15.2) - 1.375823 * jax.random.uniform(key_list[21], (H * HD, D), jnp.float32) ** block_levels(key_list[21], (H * HD, D), ((0, 8),), -0.2, 0.2)), 3.84, 15.2)
    second_gate = jnp.clip(jnp.exp(math.log(622.592) - 1.3862944 * jax.random.uniform(key_list[22], (D, FF), jnp.float32) ** block_levels(key_list[22], (D, FF), ((0, 8),), -0.2, 0.2)), 155.648, 622.592)
    second_up = jnp.clip(jnp.exp(math.log(622.592) - 1.3862944 * jax.random.uniform(key_list[23], (D, FF), jnp.float32) ** block_levels(key_list[23], (D, FF), ((0, 8),), -0.2, 0.2)), 155.648, 622.592)
    second_down = jnp.clip(jnp.exp(math.log(622.592) - 1.3862944 * jax.random.uniform(key_list[24], (FF, D), jnp.float32) ** block_levels(key_list[24], (FF, D), ((0, 8),), -0.2, 0.2)), 155.648, 622.592)
    second_gains = jnp.clip(jnp.exp(math.log(2949.12) - 1.3862944 * jax.random.uniform(key_list[25], (D + HD, 2), jnp.float32) ** block_levels(key_list[25], (D + HD, 2), ((0, 8),), -0.2, 0.2)), 737.28, 2949.12)
    return dict(tokens=tokens, cotangent=cotangent, query_weight=query_weight, key_weight=key_weight, value_weight=value_weight, output_weight=output_weight, gate_weight=gate_weight, up_weight=up_weight, down_weight=down_weight, norm_gains=norm_gains, first_query=first_query, first_key=first_key, first_value=first_value, first_output=first_output, first_gate=first_gate, first_up=first_up, first_down=first_down, first_gains=first_gains, second_query=second_query, second_key=second_key, second_value=second_value, second_output=second_output, second_gate=second_gate, second_up=second_up, second_down=second_down, second_gains=second_gains)


@jax.custom_vjp
def low(v):
    return lax.optimization_barrier(v.astype(jnp.bfloat16)).astype(jnp.float32)

@jax.custom_vjp
def low_back(v):
    return v

def low_keep(v):
    return (low(v), None)

def low_pass(kept, grad):
    return (grad,)

def back_keep(v):
    return (v, None)

def back_low(kept, grad):
    return (low(grad),)
low.defvjp(low_keep, low_pass)
low_back.defvjp(back_keep, back_low)
norm_eps = 1e-05
rope_base = 1000000.0
score_scale = 0.125
beta_one = 0.9
beta_two = 0.95
adam_eps = 1e-08

def matmul(left, right):
    return jnp.dot(left, right, preferred_element_type=jnp.float32, precision=lax.Precision.HIGHEST)

def rms_scale(values):
    return lax.rsqrt(lax.optimization_barrier(jnp.mean(values * values, axis=-1, keepdims=True)) + norm_eps)

def rotary_tables(start, count, head_dim):
    half = head_dim // 2
    inverse = jnp.power(jnp.float32(rope_base), -(jnp.arange(half).astype(jnp.float32) * 2.0) / head_dim)
    angle = (start + jnp.arange(count)).astype(jnp.float32)[:, None] * inverse[None, :]
    return (jnp.cos(angle), jnp.sin(angle))

def rotate(values, cosine, sine):
    half = values.shape[-1] // 2
    first = values[..., :half]
    second = values[..., half:]
    cosine = cosine[:, None, :]
    sine = sine[:, None, :]
    return jnp.concatenate([first * cosine - second * sine, second * cosine + first * sine], axis=-1)

def attend(queries, keys, values):
    block = math.gcd(SEQ, 512)
    group = H // KV
    blocks = queries.reshape(SEQ // block, block, KV, group, HD)
    starts = jnp.arange(SEQ // block).astype(jnp.int32) * block
    key_pos = jnp.arange(SEQ).astype(jnp.int32)

    def one_block(pair):
        query_block, start = pair
        scores = jnp.einsum('qgjd,kgd->gjqk', query_block, keys, precision=lax.Precision.HIGHEST) * score_scale
        scores = low_back(scores)
        query_pos = start + jnp.arange(block).astype(jnp.int32)
        visible = key_pos[None, :] <= query_pos[:, None]
        scores = jnp.where(visible, scores, -1e+30)
        top = lax.optimization_barrier(jnp.max(scores, axis=-1, keepdims=True))
        expo = jnp.exp(scores - top)
        probs = low(expo / lax.optimization_barrier(jnp.sum(expo, axis=-1, keepdims=True)))
        result = jnp.einsum('gjqk,kgd->qgjd', probs, values, precision=lax.Precision.HIGHEST)
        return result.reshape(block, H * HD)
    return lax.map(jax.checkpoint(one_block), (blocks, starts)).reshape(SEQ, H * HD)

def forward(inputs, query_weight, key_weight, value_weight, output_weight, gate_weight, up_weight, down_weight, norm_gains):
    gains = low(norm_gains)
    w_query = low(query_weight)
    w_key = low(key_weight)
    w_value = low(value_weight)
    w_output = low(output_weight)
    w_gate = low(gate_weight)
    w_up = low(up_weight)
    w_down = low(down_weight)
    gain_attn = gains[:D, 0]
    gain_ffn = gains[:D, 1]
    gain_query = gains[D:, 0]
    gain_key = gains[D:, 1]
    normed_one = low(inputs * rms_scale(inputs) * gain_attn)
    query_lin = low_back(matmul(normed_one, w_query))
    key_lin = low_back(matmul(normed_one, w_key))
    values = low(low_back(matmul(normed_one, w_value))).reshape(SEQ, KV, HD)
    cosine, sine = rotary_tables(0, SEQ, HD)
    query_heads = query_lin.reshape(SEQ, H, HD)
    queries = low(rotate(query_heads * rms_scale(query_heads) * gain_query, cosine, sine))
    key_heads = key_lin.reshape(SEQ, KV, HD)
    keys = low(rotate(key_heads * rms_scale(key_heads) * gain_key, cosine, sine))
    attended = low(low_back(attend(queries, keys, values)))
    resid = inputs + low_back(matmul(attended, w_output))
    normed_two = low(resid * rms_scale(resid) * gain_ffn)
    gate = low_back(matmul(normed_two, w_gate))
    up = low_back(matmul(normed_two, w_up))
    hidden = low(jax.nn.silu(gate) * up)
    return resid + low_back(matmul(hidden, w_down))

def adamw(weight, grad, first, second, rate, decay):
    first_new = beta_one * first + (1.0 - beta_one) * grad
    second_new = beta_two * second + (1.0 - beta_two) * grad * grad
    fix_one = 1.0 - beta_one ** STEP
    fix_two = 1.0 - beta_two ** STEP
    update = first_new / fix_one / (jnp.sqrt(second_new / fix_two) + adam_eps)
    return (weight - rate * (update + decay * weight), first_new, second_new)

def reference(tokens, cotangent, query_weight, key_weight, value_weight, output_weight, gate_weight, up_weight, down_weight, norm_gains, first_query, first_key, first_value, first_output, first_gate, first_up, first_down, first_gains, second_query, second_key, second_value, second_output, second_gate, second_up, second_down, second_gains):
    weights = (query_weight, key_weight, value_weight, output_weight, gate_weight, up_weight, down_weight, norm_gains)

    def per_sequence(totals, pair):
        inputs, back = pair
        result, pull = jax.vjp(forward, inputs.astype(jnp.float32), *weights)
        grads = pull(back.astype(jnp.float32))
        totals = tuple((a + b for a, b in zip(totals, grads[1:])))
        return (totals, (result.astype(jnp.bfloat16), grads[0]))
    zeros = tuple((jnp.zeros(w.shape, jnp.float32) for w in weights))
    grads, outputs = lax.scan(per_sequence, zeros, (tokens, cotangent))
    activations, input_gradient = outputs
    firsts = (first_query, first_key, first_value, first_output, first_gate, first_up, first_down, first_gains)
    seconds = (second_query, second_key, second_value, second_output, second_gate, second_up, second_down, second_gains)
    rates = (0.05, 0.05, 0.05, 0.3, 0.05, 0.05, 0.05, 0.5)
    decays = (0.1, 0.1, 0.1, 0.1, 0.1, 0.1, 0.1, 0.0)
    updated = [adamw(w, g, m, u, rate, decay) for w, g, m, u, rate, decay in zip(weights, grads, firsts, seconds, rates, decays)]
    return (activations, input_gradient, updated[0][0], updated[1][0], updated[2][0], updated[3][0], updated[4][0], updated[5][0], updated[6][0], updated[7][0], updated[0][1], updated[1][1], updated[2][1], updated[3][1], updated[4][1], updated[5][1], updated[6][1], updated[7][1], updated[0][2], updated[1][2], updated[2][2], updated[3][2], updated[4][2], updated[5][2], updated[6][2], updated[7][2])
```

```python
import functools

import jax
import jax.numpy as jnp
import numpy as np
from jax import lax
from jax.experimental import pallas as pl
from jax.experimental.pallas import tpu as pltpu
from jax.sharding import PartitionSpec as P

MESH = pl.DeviceIdType.MESH
ANY = pl.BlockSpec(memory_space=pltpu.HBM)
VMEM = pl.BlockSpec(memory_space=pltpu.VMEM)
VMEM_BYTES = 60 * 1024 * 1024

HD = 64
STEP = 5


norm_eps = 1e-05
rope_base = 1000000.0
score_scale = 0.125
beta_one = 0.9
beta_two = 0.95
adam_eps = 1e-08


def product(left, right):
    return jnp.dot(left, right, preferred_element_type=jnp.float32)


def product_back(left, right):
    return lax.dot_general(
        left, right, (((1,), (1,)), ((), ())), preferred_element_type=jnp.float32
    )


def product_rows(left, right):
    return lax.dot_general(
        left, right, (((0,), (0,)), ((), ())), preferred_element_type=jnp.float32
    )


def rms_scale(values):
    return lax.rsqrt(jnp.mean(values * values, axis=-1, keepdims=True) + norm_eps)


def norm_back(grad, values, gain):
    scale = rms_scale(values)
    scaled = grad * gain
    inner = jnp.mean(scaled * values, axis=-1, keepdims=True)
    return (scale * scaled - values * (scale * scale * scale) * inner, grad * values * scale)


def rotary_tables(start, count, head_dim):
    half = head_dim // 2
    inverse = jnp.power(
        jnp.float32(rope_base), -(jnp.arange(half).astype(jnp.float32) * 2.0) / head_dim
    )
    angle = (start + jnp.arange(count)).astype(jnp.float32)[:, None] * inverse[None, :]
    return (jnp.cos(angle), jnp.sin(angle))


def rotary_constants(count, head_dim, seqs):
    half = head_dim // 2
    inverse = np.float32(rope_base) ** -(np.arange(half).astype(np.float32) * np.float32(2.0) / np.float32(head_dim))
    angle = np.arange(count).astype(np.float32)[:, None] * inverse.astype(np.float32)[None, :]
    cosine, sine = np.cos(angle), np.sin(angle)
    return (
        np.concatenate([cosine, cosine] * seqs, axis=1).astype(np.float32),
        np.concatenate([-sine, sine] * seqs, axis=1).astype(np.float32),
    )


def rotate(values, cosine, sine):
    half = values.shape[-1] // 2
    first = values[..., :half]
    second = values[..., half:]
    cosine = cosine[:, None, :]
    sine = sine[:, None, :]
    return jnp.concatenate(
        [first * cosine - second * sine, second * cosine + first * sine], axis=-1
    )


def rotate_back(grads, cosine, sine):
    half = grads.shape[-1] // 2
    first = grads[..., :half]
    second = grads[..., half:]
    cosine = cosine[:, None, :]
    sine = sine[:, None, :]
    return jnp.concatenate(
        [first * cosine + second * sine, second * cosine - first * sine], axis=-1
    )


def adamw(weight, grad, first, second, rate, decay):
    first_new = beta_one * first + (1.0 - beta_one) * grad
    second_new = beta_two * second + (1.0 - beta_two) * grad * grad
    fix_one = 1.0 - beta_one**STEP
    fix_two = 1.0 - beta_two**STEP
    update = first_new / fix_one / (jnp.sqrt(second_new / fix_two) + adam_eps)
    return (weight - rate * (update + decay * weight), first_new, second_new)


def swap(blocks):
    return lax.all_to_all(blocks, "ctx", 0, 0)


def gather(block):
    return lax.all_gather(block, "ctx", axis=0, tiled=False)


def scatter_sum(blocks):
    return lax.psum_scatter(blocks, "ctx", scatter_dimension=0, tiled=False)


def rep_sum(values):
    return lax.psum(values, "rep")


def rep_pairs(bit):
    return [(i, i ^ bit) for i in range(lax.axis_size("rep"))]


def rep_fold(total, bit):
    low = jnp.bfloat16
    mine = (lax.axis_index("rep") // bit) % 2
    pairs = total.reshape((total.shape[0] // 2, 2) + total.shape[1:])
    keep = lax.dynamic_index_in_dim(pairs, mine, 1, keepdims=False)
    give = lax.dynamic_index_in_dim(pairs, 1 - mine, 1, keepdims=False).astype(low)
    got = lax.ppermute(give, "rep", rep_pairs(bit))
    return keep.astype(jnp.float32) + got.astype(jnp.float32)


def rep_scatter(total, bit=1):
    while total.shape[0] > 1:
        total = rep_fold(total, bit)
        bit *= 2
    return total[0].astype(jnp.bfloat16)


def rep_gather(block):
    whole = block[None]
    bit = lax.axis_size("rep") // 2
    while bit > 0:
        mine = (lax.axis_index("rep") // bit) % 2
        got = lax.ppermute(whole, "rep", rep_pairs(bit))
        first = jnp.where(mine == 0, whole, got)
        second = jnp.where(mine == 0, got, whole)
        whole = jnp.stack([first, second], axis=1).reshape((-1,) + block.shape)
        bit //= 2
    return whole


def ring_place(index, n):
    deep = lax.div(index, 2)
    side = lax.rem(index, 2)
    return deep + side * (n - 1 - 2 * deep)


def ring_index(place, n):
    side = lax.div(place, n // 2)
    deep = place + side * (n - 1 - 2 * place)
    return 2 * deep + side


def around(place, hops, n):
    return ring_index(lax.rem(place + hops + 2 * n, n), n)


def greet(others, partners=()):
    barrier = pltpu.get_barrier_semaphore()
    for other in others:
        pl.semaphore_signal(barrier, inc=1, device_id={"ctx": other}, device_id_type=MESH)
    for other in partners:
        pl.semaphore_signal(barrier, inc=1, device_id={"rep": other}, device_id_type=MESH)
    pl.semaphore_wait(barrier, len(others) + len(partners))


def remote(source, target, send, recv, other, axis="ctx"):
    return pltpu.make_async_remote_copy(
        src_ref=source,
        dst_ref=target,
        send_sem=send,
        recv_sem=recv,
        device_id={axis: other},
        device_id_type=MESH,
    )


def rep_partners():
    place = lax.axis_index("rep")
    return place + 1 - 2 * lax.rem(place, 2), lax.rem(place + 2, 4)


class RepShare:
    def __init__(self, pieces, send, recv, own_sem):
        self.pieces, self.send, self.recv, self.own_sem = pieces, send, recv, own_sem
        self.core, self.across = rep_partners()
        self.place = lax.axis_index("rep")
        self.beyond = lax.rem(self.core + 2, 4)

    def copy(self, at, which):
        source, target = self.pieces[at]
        there = target(self.across if which == 2 else self.place)
        return remote(
            there if which == 2 else source,
            there,
            self.send.at[at, which],
            self.recv.at[at, which],
            self.across if which == 0 else self.core,
            "rep",
        )

    def own(self, at):
        source, target = self.pieces[at]
        return pltpu.make_async_copy(source, target(self.place), self.own_sem.at[at])

    def arrival(self, at, which):
        _, target = self.pieces[at]
        there = target((self.across, self.core, self.beyond)[which])
        return remote(
            there, there, self.send.at[at, which], self.recv.at[at, which], self.core, "rep"
        )

    def begin(self):
        for at in range(len(self.pieces)):
            self.copy(at, 0).start()
            self.copy(at, 1).start()
            self.own(at).start()

    def middle(self, only=None):
        for at in range(len(self.pieces)) if only is None else (only,):
            self.arrival(at, 0).wait_recv()
            self.copy(at, 2).start()

    def end(self):
        for at in range(len(self.pieces)):
            self.own(at).wait()
            for which in range(3):
                if which > 0:
                    self.arrival(at, which).wait_recv()
                self.copy(at, which).wait_send()


def add_into(total, other, step):
    @pl.loop(0, total.shape[0] // step)
    def _(at):
        here = pl.ds(pl.multiple_of(at * step, step), step)
        summed = total[here].astype(jnp.float32) + other[here].astype(jnp.float32)
        total[here] = summed.astype(total.dtype)


def add_columns(total, other, step):
    @pl.loop(0, total.shape[1] // step)
    def _(at):
        here = pl.ds(pl.multiple_of(at * step, step), step)
        summed = total[:, here].astype(jnp.float32) + other[:, here].astype(jnp.float32)
        total[:, here] = summed.astype(total.dtype)


def entry_kernel(n, head_dim, x_ref, g_ref, wq_ref, wk_ref, wv_ref, wo_ref, wg_ref, wu_ref, *refs):
    wd_ref, h_out, lin_out, g_out, o_out, q_out, wg_out, wu_out, wd_out = refs[:9]
    x_all, h_all, w_all, gain, mixed, q_own, o_own, f_own = refs[9:17]
    wq, wk, wv, wo, wf, wd, f_all, wd_low = refs[17:25]
    x_send, x_recv, p_send, p_recv, own_sem, load_sem, h_sem, r_send, r_recv, r_own = refs[25:]
    f32, low = jnp.float32, jnp.bfloat16
    me = lax.axis_index("ctx")
    place = ring_place(me, n)
    others = [lax.rem(me + hop, n) for hop in range(1, n)]
    right, left = around(place, 1, n), around(place, -1, n)
    quarter = x_ref.shape[0] // 4
    span = x_ref.shape[0] // 2
    width = x_ref.shape[1]
    share = o_own.shape[0]
    rep_rows = pl.ds(pl.multiple_of(lax.axis_index("rep") * share, 16), share)
    loads = [
        pltpu.make_async_copy(source, target, load_sem.at[at])
        for at, (source, target) in enumerate(
            (
                (wq_ref, wq),
                (wk_ref, wk),
                (wv_ref, wv),
                (wo_ref.at[rep_rows], wo),
                (wg_ref.at[rep_rows], wf.at[0]),
                (wu_ref.at[rep_rows], wf.at[1]),
                (wd_ref, wd),
            )
        )
    ]
    for at in (4, 5, 0, 1, 2, 3, 6):
        loads[at].start()
    pieces = [(x_ref, x_all, (pl.ds(part * quarter, quarter),), part < 2) for part in (0, 2, 1, 3)]
    for source, target in ((o_own, o_out), (q_own, q_out)):
        wide = source.shape[1] // 2
        pieces += [
            (source, target, (slice(None), pl.ds(part * wide, wide)), part < 1) for part in (0, 1)
        ]
    tokens, weights = range(4), range(4, len(pieces))

    def owner_of(step, up):
        return around(place, -1 - step if up else 1 + step, n)

    def hop_copy(at, step):
        source, target, where, up = pieces[at]
        owner = owner_of(step, up)
        first = isinstance(step, int) and step < 0
        return remote(
            source.at[where] if first else target.at[(owner,) + where],
            target.at[(owner,) + where],
            x_send.at[at, step + 1],
            x_recv.at[at, step + 1],
            right if up else left,
        )

    def arrived(at, step):
        _, target, where, up = pieces[at]
        block = target.at[(owner_of(step, up),) + where]
        remote(block, block, x_send.at[at, step], x_recv.at[at, step], right).wait_recv()

    def pass_first(step):
        for at in range(len(pieces)):
            arrived(at, step)
            hop_copy(at, step).start()

    def pass_on(which, step):
        @pl.when(step < n - 1)
        def _():
            for at in which:
                arrived(at, step)

                @pl.when(step < n - 2)
                def _():
                    hop_copy(at, step).start()

    def swap_copy(at, hop):
        other = others[hop - 1]
        source, target = (
            (mixed.at[other], w_all.at[me]),
            (g_ref, g_out.at[me]),
            (f_own.at[other], f_all.at[:, me]),
        )[at]
        return remote(source, target, p_send.at[at, hop], p_recv.at[at, hop], other)

    own = [
        pltpu.make_async_copy(source, target, own_sem.at[at])
        for at, (source, target) in enumerate(
            (
                (x_ref, x_all.at[me]),
                (g_ref, g_out.at[me]),
                (mixed.at[me], w_all.at[me]),
                (o_own, o_out.at[me]),
                (q_own, q_out.at[me]),
                (f_own.at[me], f_all.at[:, me]),
            )
        )
    ]
    share_feed = RepShare(
        [
            (f_all.at[0], lambda r: wg_out.at[:, r]),
            (f_all.at[1], lambda r: wu_out.at[:, r]),
        ],
        r_send,
        r_recv,
        r_own,
    )
    own[0].start()
    own[1].start()
    greet(others, rep_partners())
    for at in tokens:
        hop_copy(at, -1).start()
    for copy in loads[4:6]:
        copy.wait()
    wide = f_own.shape[3]
    for owner in range(n):
        for at in (0, 1):
            f_own[owner, at] = wf[at, :, owner * wide : (owner + 1) * wide].astype(low)
    own[5].start()
    for hop in range(1, n):
        swap_copy(2, hop).start()
    for copy in loads[:3]:
        copy.wait()
    for source, at, wide in ((wq, 0, wq.shape[1] // n), (wk, 1, head_dim), (wv, 2, head_dim)):
        start = (0, wq.shape[1] // n, wq.shape[1] // n + head_dim)[at]
        for owner in range(n):
            mixed[owner, :, start : start + wide] = source[
                :, owner * wide : (owner + 1) * wide
            ].astype(low)
    own[2].start()
    for hop in range(1, n):
        swap_copy(0, hop).start()
        swap_copy(1, hop).start()
    columns = mixed.shape[2]
    for owner in range(n):
        q_own[:, owner * columns : (owner + 1) * columns] = mixed[owner, rep_rows]
    loads[3].wait()
    o_own[...] = wo[...].astype(low)
    own[3].start()
    own[4].start()
    for at in weights:
        hop_copy(at, -1).start()
    pass_first(0)
    loads[6].wait()

    @pl.loop(0, wd.shape[0] // 16)
    def _(at):
        here = pl.ds(pl.multiple_of(at * 16, 16), 16)
        wd_low[here] = wd[here].astype(low)

    wd_give = pltpu.make_async_copy(wd_low, wd_out, own_sem.at[6])
    wd_give.start()
    for hop in range(1, n):
        swap_copy(0, hop).wait_recv()
        swap_copy(1, hop).wait_recv()
    for copy in own[:3]:
        copy.wait()
    few = gain.shape[1] // n
    for owner in range(n):
        gain[:, owner * few : (owner + 1) * few] = g_out[owner, :, :few]
    heads = lin_out.shape[0]

    def give_out(step, seq):
        owner = owner_of(step, seq == 0)
        return pltpu.make_async_copy(h_all.at[owner, seq], h_out.at[owner, seq], h_sem.at[seq, step])

    def multiply(step, seq):
        owner = owner_of(step, seq == 0)
        x = x_all[owner, pl.ds(seq * span, span)].astype(f32)
        normed = (x * rms_scale(x) * gain[0:1, :width]).astype(low)
        h_all[owner, seq] = normed
        give_out(step, seq).start()
        lin = product(normed, w_all[...].reshape(width, -1))
        rows = pl.ds(pl.multiple_of(owner * span, span), span)
        for head in range(heads):
            lin_out[head, rows, seq * head_dim : (seq + 1) * head_dim] = lin[
                :, head * head_dim : (head + 1) * head_dim
            ]

    multiply(n - 1, 0)
    multiply(n - 1, 1)

    @pl.loop(0, n - 1)
    def _(step):
        pass_on(tokens, step + 1)
        multiply(step, 0)
        pass_on(weights, step + 1)

        @pl.when(step == 2)
        def _():
            own[5].wait()
            for hop in range(1, n):
                swap_copy(2, hop).wait_recv()
            share_feed.begin()

        @pl.when(step == n - 2)
        def _():
            share_feed.middle()

        multiply(step, 1)

    wd_give.wait()
    for copy in own[3:5]:
        copy.wait()
    for at in range(len(pieces)):
        hop_copy(at, -1).wait_send()

        @pl.loop(0, n - 2)
        def _(step):
            hop_copy(at, step).wait_send()

    @pl.loop(0, n)
    def _(step):
        give_out(step, 0).wait()
        give_out(step, 1).wait()

    for hop in range(1, n):
        swap_copy(0, hop).wait_send()
        swap_copy(1, hop).wait_send()
        swap_copy(2, hop).wait_send()
    share_feed.end()


def enter(block, gains, shards, feed_shards, w_down, head_dim):
    n = lax.axis_size("ctx")
    rows, width = block.shape
    f32, low = jnp.float32, jnp.bfloat16
    shard, q_width = shards[0].shape
    kv_width = shards[1].shape[1]
    out_width = shards[3].shape[1]
    reps = lax.axis_size("rep")
    few = shard // reps
    all_width = q_width + 2 * kv_width
    feed_width = feed_shards[0].shape[1]
    return pl.pallas_call(
        functools.partial(entry_kernel, n, head_dim),
        out_shape=[
            jax.ShapeDtypeStruct((n, 2, rows // 2, width), low),
            jax.ShapeDtypeStruct((all_width // n // head_dim, n * rows // 2, 2 * head_dim), f32),
            jax.ShapeDtypeStruct((n,) + gains.shape, f32),
            jax.ShapeDtypeStruct((n, few, out_width), low),
            jax.ShapeDtypeStruct((n, few, all_width), low),
            jax.ShapeDtypeStruct((n, reps, few, feed_width // n), low),
            jax.ShapeDtypeStruct((n, reps, few, feed_width // n), low),
            jax.ShapeDtypeStruct(w_down.shape, low),
        ],
        in_specs=[ANY] * 9,
        out_specs=[ANY, VMEM, VMEM, ANY, ANY, ANY, ANY, ANY],
        scratch_shapes=[
            pltpu.VMEM((n, rows, width), low),
            pltpu.VMEM((n, 2, rows // 2, width), low),
            pltpu.VMEM((n, shard, all_width // n), low),
            pltpu.VMEM((gains.shape[0], width + head_dim), f32),
            pltpu.VMEM((n, shard, all_width // n), low),
            pltpu.VMEM((few, all_width), low),
            pltpu.VMEM((few, out_width), low),
            pltpu.VMEM((n, 2, few, feed_width // n), low),
            pltpu.VMEM((shard, q_width), f32),
            pltpu.VMEM((shard, kv_width), f32),
            pltpu.VMEM((shard, kv_width), f32),
            pltpu.VMEM((few, out_width), f32),
            pltpu.VMEM((2, few, feed_width), f32),
            pltpu.VMEM(w_down.shape, f32),
            pltpu.VMEM((2, n, few, feed_width // n), low),
            pltpu.VMEM(w_down.shape, low),
            pltpu.SemaphoreType.DMA((8, n)),
            pltpu.SemaphoreType.DMA((8, n)),
            pltpu.SemaphoreType.DMA((3, n)),
            pltpu.SemaphoreType.DMA((3, n)),
            pltpu.SemaphoreType.DMA((7,)),
            pltpu.SemaphoreType.DMA((7,)),
            pltpu.SemaphoreType.DMA((2, n)),
            pltpu.SemaphoreType.DMA((2, 3)),
            pltpu.SemaphoreType.DMA((2, 3)),
            pltpu.SemaphoreType.DMA((2,)),
        ],
        compiler_params=pltpu.CompilerParams(
            collective_id=0, has_side_effects=True, vmem_limit_bytes=VMEM_BYTES
        ),
    )(block, gains, *shards, *feed_shards, w_down)


def lane_half(shape):
    return lax.broadcasted_iota(jnp.int32, shape, len(shape) - 1) < shape[-1] // 2


def pack(first, second):
    return jnp.where(lane_half(first.shape), first, second)


def half_mean(values):
    left = lane_half(values.shape)
    one = jnp.sum(jnp.where(left, values, 0.0), axis=-1, keepdims=True)
    two = jnp.sum(jnp.where(left, 0.0, values), axis=-1, keepdims=True)
    return jnp.where(left, one, two) * (2.0 / values.shape[-1])


def half_turn(values):
    wide = values.shape[-1]
    lane = lax.broadcasted_iota(jnp.int32, values.shape, len(values.shape) - 1)
    axis = len(values.shape) - 1
    return jnp.where(
        lax.rem(lane, wide // 2) < wide // 4,
        pltpu.roll(values, wide - wide // 4, axis),
        pltpu.roll(values, wide // 4, axis),
    )


def side_by_side(blocks, flat):
    n, count, span, wide = blocks.shape
    half = wide // 2
    left = lane_half((span, wide))

    @pl.loop(0, n // 2)
    def _(pair):
        heads = [blocks[2 * pair + at, head].astype(jnp.float32) for at in (0, 1) for head in range(count)]
        for at in range(count):
            one, two = heads[2 * at], heads[2 * at + 1]
            cols = pl.ds(pl.multiple_of((pair * count + at) * wide, wide), wide)
            flat[0:span, cols] = jnp.where(left, one, pltpu.roll(two, half, 1)).astype(flat.dtype)
            flat[span : 2 * span, cols] = jnp.where(left, pltpu.roll(one, half, 1), two).astype(
                flat.dtype
            )


def masked(scores):
    block, keys = scores.shape
    row = lax.broadcasted_iota(jnp.int32, (block, block), 0)
    seen = lax.broadcasted_iota(jnp.int32, (block, block), 1) <= row
    last = jnp.where(seen, scores[:, keys - block :], -1e30)
    return last if keys == block else jnp.concatenate([scores[:, : keys - block], last], axis=1)


def scaled(queries):
    return (queries.astype(jnp.float32) * score_scale).astype(queries.dtype)


def halves(packed):
    left = lane_half(packed.shape)
    zero = jnp.zeros_like(packed)
    return jnp.where(left, packed, zero), jnp.where(left, zero, packed)


def attend_kernel(n, group, block, lin_ref, cos_ref, sin_ref, gain_ref, x_ref, norm_ref, *refs):
    dy_ref, wo_ref = refs[:2]
    low_give, lse_give, flat_out, resid_out, next_out, dy_give, wo_out = refs[2:9]
    o_own, o_out, w_all, low_out, lse_out, dy_out = refs[9:15]
    o_send, o_recv, dy_send, dy_recv, r_send, r_recv, r_own, own_sem = refs[15:]
    f32, low = jnp.float32, jnp.bfloat16
    me = lax.axis_index("ctx")
    place = ring_place(me, n)
    others = [lax.rem(me + hop, n) for hop in range(1, n)]
    toward = (around(place, 1, n), around(place, -1, n))
    length = lin_ref.shape[1]
    span = length // n
    rows = dy_ref.shape[0] // 2
    parts = (pl.ds(0, rows), pl.ds(rows, rows))
    share = RepShare(
        [(wo_ref, lambda r: wo_out.at[:, r])],
        r_send,
        r_recv,
        r_own,
    )
    greet(others, rep_partners())

    def ring(step, side):
        owner = around(place, -step if side == 0 else step, n)
        there = dy_out.at[owner, parts[side]]
        return remote(
            there, there, dy_send.at[side, step], dy_recv.at[side, step], toward[side]
        )

    def first(side):
        return remote(
            dy_ref.at[parts[side]],
            dy_out.at[me, parts[side]],
            dy_send.at[side, 0],
            dy_recv.at[side, 0],
            toward[side],
        )

    def hop_on(step):
        for side in (0, 1):
            owner = around(place, -1 - step if side == 0 else 1 + step, n)
            there = dy_out.at[owner, parts[side]]
            remote(
                there, there, dy_send.at[side, step], dy_recv.at[side, step], toward[side]
            ).wait_recv()

            @pl.when(step < n - 2)
            def _():
                ring(step + 1, side).start()

    def give(head, hop):
        return remote(
            o_own.at[head, pl.ds(pl.multiple_of(others[hop - 1] * span, span), span)],
            o_out.at[me, head],
            o_send.at[head, hop],
            o_recv.at[head, hop],
            others[hop - 1],
        )

    for side in (0, 1):
        first(side).start()
    share.begin()
    keep_dy = pltpu.make_async_copy(dy_ref, dy_out.at[me], own_sem.at[0])
    keep_dy.start()

    for head in range(group + 1):

        @pl.loop(0, length // block)
        def _(at):
            here = pl.ds(pl.multiple_of(at * block, block), block)
            u = lin_ref[head, here]
            gain = gain_ref[0:1] if head < group else gain_ref[1:2]
            z = u * lax.rsqrt(half_mean(u * u) + norm_eps) * gain
            low_out[head, here] = (z * cos_ref[here] + half_turn(z) * sin_ref[here]).astype(low)
            if head == group:
                low_out[group + 1, here] = lin_ref[group + 1, here].astype(low)

    @pl.loop(0, group)
    def _(head):
        for at in range(length // block):
            keys = (at + 1) * block
            here = pl.ds(at * block, block)
            outs, sums = [], []
            for query in halves(scaled(low_out[head, here])):
                scores = masked(product_back(query, low_out[group, :keys]))
                top = jnp.max(scores, axis=-1, keepdims=True)
                expo = jnp.exp(scores - top)
                total = jnp.sum(expo, axis=-1, keepdims=True)
                probs = (expo * (1.0 / total)).astype(low)
                outs.append(product(probs, low_out[group + 1, :keys]))
                sums.append(jnp.broadcast_to(top + jnp.log(total), (block, low_out.shape[2])))
            o_own[head, here] = pack(*outs).astype(low)
            lse_out[head, here] = pack(*sums)
            for unit in range(2, group * (length // block), 3):
                if unit % (length // block) == at:

                    @pl.when(head == unit // (length // block))
                    def _(unit=unit):
                        hop_on(unit // 3)

        for hop in range(1, n):
            give(head, hop).start()

    gives = [
        pltpu.make_async_copy(source, target, own_sem.at[3 + at])
        for at, (source, target) in enumerate(
            ((low_out, low_give), (lse_out, lse_give), (dy_out, dy_give))
        )
    ]
    gives[0].start()
    gives[1].start()
    served = group * (length // block) // 3
    middle = served + 1

    @pl.loop(served, middle)
    def _(step):
        hop_on(step)

    share.middle()

    @pl.loop(middle, n - 1)
    def _(step):
        hop_on(step)

    keep_dy.wait()
    gives[2].start()
    keep_o = pltpu.make_async_copy(
        o_own.at[:, pl.ds(pl.multiple_of(me * span, span), span)], o_out.at[me], own_sem.at[1]
    )
    keep_o.start()
    for side in (0, 1):
        first(side).wait_send()

        @pl.loop(1, n - 1)
        def _(step):
            ring(step, side).wait_send()

    @pl.loop(0, group)
    def _(head):
        for hop in range(1, n):
            give(head, hop).wait_send()
            source = lax.rem(me + n - hop, n)
            there = o_out.at[source, head]
            remote(
                there, there, o_send.at[head, hop], o_recv.at[head, hop], others[hop - 1]
            ).wait_recv()

    keep_o.wait()
    side_by_side(o_out, flat_out)
    share.end()
    fetch = pltpu.make_async_copy(wo_out, w_all, own_sem.at[2])
    fetch.start()
    fetch.wait()
    weights = w_all[...].reshape(-1, w_all.shape[3])
    x = x_ref[...].astype(f32)
    resid = x + product(flat_out[...], weights)
    resid_out[...] = resid
    next_out[...] = (resid * rms_scale(resid) * norm_ref[...]).astype(low)
    for copy in gives:
        copy.wait()


def attend(lin, cosine, sine, gain, tokens, norm_gain, grad, w_out):
    n = lax.axis_size("ctx")
    reps = lax.axis_size("rep")
    f32, low = jnp.float32, jnp.bfloat16
    count, length, wide = lin.shape
    group = count - 2
    return pl.pallas_call(
        functools.partial(attend_kernel, n, group, 256),
        out_shape=[
            jax.ShapeDtypeStruct((count, length, wide), low),
            jax.ShapeDtypeStruct((group, length, wide), f32),
            jax.ShapeDtypeStruct(tokens.shape, low),
            jax.ShapeDtypeStruct(tokens.shape, f32),
            jax.ShapeDtypeStruct(tokens.shape, low),
            jax.ShapeDtypeStruct((n,) + grad.shape, low),
            jax.ShapeDtypeStruct((n, reps) + w_out.shape[1:], low),
        ],
        in_specs=[VMEM] * 6 + [ANY] * 2,
        out_specs=[ANY] * 2 + [VMEM] * 3 + [ANY] * 2,
        scratch_shapes=[
            pltpu.VMEM((group, length, wide), low),
            pltpu.VMEM((n, group, length // n, wide), low),
            pltpu.VMEM((n, reps) + w_out.shape[1:], low),
            pltpu.VMEM((count, length, wide), low),
            pltpu.VMEM((group, length, wide), f32),
            pltpu.VMEM((n,) + grad.shape, low),
            pltpu.SemaphoreType.DMA((group, n)),
            pltpu.SemaphoreType.DMA((group, n)),
            pltpu.SemaphoreType.DMA((2, n)),
            pltpu.SemaphoreType.DMA((2, n)),
            pltpu.SemaphoreType.DMA((1, 3)),
            pltpu.SemaphoreType.DMA((1, 3)),
            pltpu.SemaphoreType.DMA((1,)),
            pltpu.SemaphoreType.DMA((6,)),
        ],
        compiler_params=pltpu.CompilerParams(
            collective_id=2, has_side_effects=True, vmem_limit_bytes=VMEM_BYTES
        ),
        cost_estimate=pl.CostEstimate(
            flops=16 * group * length * length * wide, bytes_accessed=2**26, transcendentals=0
        ),
    )(lin, cosine, sine, gain, tokens, norm_gain, grad, w_out)


def attend_back_kernel(n, group, block, low_src, lse_src, lin_src, cos_src, sin_src, gain_ref, b_ref, r_ref, dy_ref, *refs):
    f_ref, att_ref, wo_ref = refs[:3]
    g_keep, g_got, u_keep, u_got, d_keep, d_got, h_ref = refs[3:10]
    d_out, q_out, g_out, g_give, u_give, d_give, o_give, dr_out, f_out = refs[10:19]
    do_own, do_all, dk_sum, dv_sum, g1, g2, g3, u1, u2, u3, d1, d2, o_term, o2 = refs[19:33]
    d_own, g_swap, u_swap, h_all, q_term, q2, q_sum, g_flat, u_flat, d_sum, o_sum = refs[33:44]
    dr_low, low_ref, lse_ref, lin_ref, cos_ref, sin_ref = refs[44:50]
    do_send, do_recv, d_send, d_recv, own_sem, load_sem, x_send, x_recv = refs[50:58]
    a_send, a_recv, give_sem, head_sem = refs[58:]
    f32, low = jnp.float32, jnp.bfloat16
    me = lax.axis_index("ctx")
    others = [lax.rem(me + hop, n) for hop in range(1, n)]
    length, wide = lin_src.shape[1:]
    span = length // n

    def owned(index):
        return pl.ds(pl.multiple_of(index * span, span), span)

    def bring(head, hop):
        return remote(
            do_own.at[others[hop - 1], head],
            do_all.at[head, owned(me)],
            do_send.at[head, hop],
            do_recv.at[head, hop],
            others[hop - 1],
        )

    def give(head, hop):
        return remote(
            d_own.at[head, owned(others[hop - 1])],
            d_out.at[me, head],
            d_send.at[head, hop],
            d_recv.at[head, hop],
            others[hop - 1],
        )

    rep_place = lax.axis_index("rep")
    mine_core, mine_x = lax.rem(rep_place, 2), lax.div(rep_place, 2)
    core, across = rep_partners()
    loads = [
        pltpu.make_async_copy(source, target, load_sem.at[at])
        for at, (source, target) in enumerate(
            (
                (d_keep, d1),
                (d_got, d2),
                (g_keep, g1),
                (g_got, g2),
                (u_keep, u1),
                (u_got, u2),
                (wo_ref.at[pl.ds(0, n)], h_all.at[0]),
                (wo_ref.at[pl.ds(n, wo_ref.shape[0] - n)], h_all.at[1, pl.ds(0, wo_ref.shape[0] - n)]),
                (h_ref.at[:, 0], h_all.at[0]),
                (h_ref.at[:, 1], h_all.at[1]),
            )
        )
    ]
    head_loads = [
        pltpu.make_async_copy(source, target, head_sem.at[at])
        for at, (source, target) in enumerate(
            (
                (low_src, low_ref),
                (lse_src, lse_ref),
                (lin_src, lin_ref),
                (cos_src, cos_ref),
                (sin_src, sin_ref),
            )
        )
    ]
    for at in (6, 7, 2, 3, 4, 5, 0, 1):
        loads[at].start()
    for copy in head_loads:
        copy.start()

    def cross(at, source, target, other):
        return remote(source, target, x_send.at[at], x_recv.at[at], other, "rep")

    def crossing(at):
        if at == 5:
            return cross(5, q_term.at[:, :, 1 - mine_core], q2, core)
        if at == 4:
            return cross(4, o_term.at[:, :, 1 - mine_core], o2, core)
        if at == 0:
            return cross(0, d1.at[1 - mine_x], d_sum, across)
        source, target = ((g1, g3), (u1, u3), (o_term, o_sum))[at - 1]
        if at == 3:
            return cross(3, o_term.at[:, 1 - mine_x, mine_core], o_sum, across)
        return cross(at, source.at[:, 1 - mine_x], target, across)

    def swap_out(at, hop):
        source, target = ((g3, g_swap), (u3, u_swap))[at]
        other = others[hop - 1]
        return remote(
            source.at[other], target.at[me], a_send.at[at, hop], a_recv.at[at, hop], other
        )

    def swap_own(at):
        source, target = ((g3, g_swap), (u3, u_swap))[at]
        return pltpu.make_async_copy(source.at[me], target.at[me], own_sem.at[2 + at])

    greet(others, rep_partners())
    chunk = 64
    totals = jnp.zeros((1, f_ref.shape[1]), f32)
    for at in range(r_ref.shape[0] // chunk):
        here = pl.ds(at * chunk, chunk)
        back, terms = norm_back(b_ref[here].astype(f32), r_ref[here], f_ref[...])
        grads = dy_ref[here].astype(f32) + back
        totals += jnp.sum(terms, axis=0, keepdims=True)
        dr_out[here] = grads
        dr_low[here] = grads.astype(low)
    f_out[...] = jnp.broadcast_to(totals, f_out.shape)
    for copy in loads[6:8]:
        copy.wait()
    left = lane_half((span, wide))

    @pl.loop(0, n // 2)
    def _(pair):
        heads = []
        for at in range(group):
            index = pair * group + at
            both = product_back(dr_low[...], h_all[lax.div(index, n), lax.rem(index, n)])
            one, two = both[:span], both[span:]
            heads.append(jnp.where(left, one, pltpu.roll(two, wide // 2, 1)))
            heads.append(jnp.where(left, pltpu.roll(one, wide // 2, 1), two))
        for at, values in enumerate(heads):
            do_own[2 * pair + at // group, at % group] = values.astype(low)

    for copy in loads[8:]:
        copy.start()
    for head in range(group):
        for hop in range(1, n):
            bring(head, hop).start()
    keep_do = pltpu.make_async_copy(do_own.at[me], do_all.at[:, owned(me)], own_sem.at[0])
    keep_do.start()
    piece = d1.shape[1] // 6
    for copy in loads[2:4]:
        copy.wait()
    add_into(g1, g2, 1)
    crossing(1).start()
    for copy in loads[4:6]:
        copy.wait()
    add_into(u1, u2, 1)
    crossing(2).start()
    for copy in loads[:2]:
        copy.wait()
    add_columns(d1, d2, piece)
    crossing(0).start()
    shard = h_all.shape[3] // n

    @pl.loop(0, n // 2)
    def _(pair):
        cols = pl.ds(pl.multiple_of(pair * 2 * shard, 2 * shard), 2 * shard)
        part = product_rows(att_ref[:, cols], dr_low[...]).astype(low)
        o_term[pl.ds(2 * pair, 2)] = part.reshape(2, 2, 2, shard // 4, part.shape[1])

    crossing(4).start()
    dk_sum[...] = jnp.zeros_like(dk_sum)
    dv_sum[...] = jnp.zeros_like(dv_sum)
    g_out[...] = jnp.zeros_like(g_out)
    keep_do.wait()

    def head_back(grad, here, head, gain_at):
        turned = grad * cos_ref[here] - half_turn(grad) * sin_ref[here]
        u = lin_ref[head, here]
        scale = lax.rsqrt(half_mean(u * u) + norm_eps)
        scaled = turned * gain_ref[gain_at : gain_at + 1]
        inner = half_mean(scaled * u)
        g_out[gain_at : gain_at + 1] += jnp.sum(turned * u * scale, axis=0, keepdims=True)
        d_own[head, here] = (scale * scaled - u * (scale * scale * scale) * inner).astype(low)

    def swap_rows(at):
        first, total = ((g1, g3), (u1, u3))[at]
        crossing(1 + at).wait_recv()

        @pl.loop(0, n)
        def _(owner):
            summed = total[owner].astype(f32) + first[owner, mine_x].astype(f32)
            total[owner] = summed.astype(low)

        swap_own(at).start()
        for hop in range(1, n):
            swap_out(at, hop).start()

    swap_rows(0)
    for copy in head_loads:
        copy.wait()

    @pl.loop(0, group)
    def _(head):
        for hop in range(1, n):
            there = do_all.at[head, owned(lax.rem(me + n - hop, n))]
            remote(
                there, there, do_send.at[head, hop], do_recv.at[head, hop], others[hop - 1]
            ).wait_recv()
        for at in range(length // block):
            keys = (at + 1) * block
            here = pl.ds(at * block, block)
            query_all, grad_all = scaled(low_ref[head, here]), do_all[head, here]
            log_all = lse_ref[head, here]
            logs = (log_all[:, 0:1], log_all[:, wide // 2 : wide // 2 + 1])
            dqs, dks, dvs = [], [], []
            for query, grad, log_sum in zip(halves(query_all), halves(grad_all), logs):
                scores = masked(product_back(query, low_ref[group, :keys]))
                probs = jnp.exp(scores - log_sum)
                grad_probs = product_back(grad, low_ref[group + 1, :keys])
                both = probs * grad_probs
                inner = jnp.sum(both, axis=-1, keepdims=True)
                grad_scores = (both - probs * inner).astype(low)
                dqs.append(product(grad_scores, low_ref[group, :keys]))
                dks.append(product_rows(grad_scores, query_all))
                dvs.append(product_rows(probs.astype(low), grad_all))
            dk_sum[:keys] += pack(*dks)
            dv_sum[:keys] += pack(*dvs)
            head_back(pack(*dqs) * score_scale, here, head, 0)
        for hop in range(1, n):
            give(head, hop).start()

        @pl.when(head == 0)
        def _():
            crossing(4).wait_recv()

            @pl.loop(0, n)
            def _(owner):
                summed = o_term[owner, :, mine_core].astype(f32) + o2[owner].astype(f32)
                o_term[owner, :, mine_core] = summed.astype(low)

            crossing(3).start()
            swap_rows(1)

    @pl.loop(0, length // block)
    def _(at):
        here = pl.ds(pl.multiple_of(at * block, block), block)
        head_back(dk_sum[here], here, group, 1)
        d_own[group + 1, here] = dv_sum[here].astype(low)

    for head in (group, group + 1):
        for hop in range(1, n):
            give(head, hop).start()
    keep_d = pltpu.make_async_copy(d_own.at[:, owned(me)], d_out.at[me], own_sem.at[1])
    keep_d.start()
    for copy in loads[8:]:
        copy.wait()

    @pl.loop(0, n // 2)
    def _(pair):
        cols = pl.ds(pl.multiple_of(pair * 2 * shard, 2 * shard), 2 * shard)
        grads = jnp.concatenate([d_own[head] for head in range(group + 2)], axis=1)
        sums = [
            product_rows(h_all[seq, :, :, cols].reshape(length, 2 * shard), grads)
            for seq in (0, 1)
        ]
        both = []
        for head in range(group + 2):
            here = slice(head * wide, (head + 1) * wide)
            packed = pack(sums[0][:, here], sums[1][:, here])
            both.append(packed + pltpu.roll(packed, wide // 2, 1))
        both.append(jnp.zeros_like(both[0]))
        for at in range(0, group + 2, 2):
            part = pack(both[at], both[at + 1]).astype(low).reshape(2, 2, 2, shard // 4, wide)
            q_term[pl.ds(2 * pair, 2), :, :, :, at // 2 * wide : (at // 2 + 1) * wide] = part

    gives = [
        pltpu.make_async_copy(source, target, give_sem.at[at])
        for at, (source, target) in enumerate(
            (
                (d_sum, d_give),
                (q_sum, q_out),
                (o_sum, o_give),
                (g_flat, g_give),
                (u_flat, u_give),
            )
        )
    ]
    crossing(5).start()
    crossing(0).wait_recv()
    piece = d1.shape[1] // 6

    @pl.loop(0, 6)
    def _(at):
        here = pl.ds(pl.multiple_of(at * piece, piece), piece)
        summed = d_sum[here].astype(f32) + d1[mine_x, here].astype(f32)
        d_sum[here] = summed.astype(low)

    gives[0].start()
    crossing(5).wait_recv()

    @pl.loop(0, n)
    def _(owner):
        summed = q_term[owner, :, mine_core].astype(f32) + q2[owner].astype(f32)
        q_sum[owner] = summed.astype(low)

    gives[1].start()
    crossing(3).wait_recv()

    @pl.loop(0, n)
    def _(owner):
        summed = o_sum[owner].astype(f32) + o_term[owner, mine_x, mine_core].astype(f32)
        o_sum[owner] = summed.astype(low)

    gives[2].start()
    for at in range(6):
        crossing(at).wait_send()
    for at in (0, 1):
        swap_own(at).wait()
        for hop in range(1, n):
            swap_out(at, hop).wait()
        swapped, flat = ((g_swap, g_flat), (u_swap, u_flat))[at]
        cols = swapped.shape[2]
        for source in range(n):
            flat[:, source * cols : (source + 1) * cols] = swapped[source]
        gives[3 + at].start()

    @pl.loop(0, group)
    def _(head):
        for hop in range(1, n):
            bring(head, hop).wait_send()

    @pl.loop(0, group + 2)
    def _(head):
        for hop in range(1, n):
            give(head, hop).wait_send()
            there = d_out.at[lax.rem(me + n - hop, n), head]
            remote(
                there, there, d_send.at[head, hop], d_recv.at[head, hop], others[hop - 1]
            ).wait_recv()

    keep_d.wait()
    for copy in gives:
        copy.wait()


def attend_back(low_heads, log_sums, lin, cosine, sine, gain, above, w_output, feed_terms, normed):
    n = lax.axis_size("ctx")
    f32, low = jnp.float32, jnp.bfloat16
    count, length, wide = lin.shape
    group = count - 2
    width = normed.shape[3]
    rows_half, cols_half = feed_terms[0].shape, feed_terms[4].shape
    rows, out_width = above[4].shape
    out_half = (n, 2, rows_half[2], width)
    return pl.pallas_call(
        functools.partial(attend_back_kernel, n, group, 256),
        out_shape=[
            jax.ShapeDtypeStruct((n, count, length // n, wide), low),
            jax.ShapeDtypeStruct((n, 2, rows_half[2], (count + 1) // 2 * wide), low),
            jax.ShapeDtypeStruct(gain.shape, f32),
            jax.ShapeDtypeStruct((rows_half[2], n * rows_half[3]), low),
            jax.ShapeDtypeStruct((rows_half[2], n * rows_half[3]), low),
            jax.ShapeDtypeStruct(cols_half[1:], low),
            jax.ShapeDtypeStruct((n,) + out_half[2:], low),
            jax.ShapeDtypeStruct((rows, width), f32),
            jax.ShapeDtypeStruct((8, width), f32),
        ],
        in_specs=[ANY] * 5 + [VMEM] * 6 + [ANY] * 8,
        out_specs=[ANY, ANY, VMEM] + [ANY] * 4 + [VMEM] * 2,
        scratch_shapes=[
            pltpu.VMEM((n, group, length // n, wide), low),
            pltpu.VMEM((group, length, wide), low),
            pltpu.VMEM((length, wide), f32),
            pltpu.VMEM((length, wide), f32),
        ]
        + [pltpu.VMEM(shape, low) for shape in (rows_half, rows_half, (n,) + rows_half[2:])] * 2
        + [pltpu.VMEM(shape, low) for shape in (cols_half, cols_half)]
        + [pltpu.VMEM((n, 2) + out_half[1:], low), pltpu.VMEM(out_half, low)]
        + [
            pltpu.VMEM((count, length, wide), low),
            pltpu.VMEM((n,) + rows_half[2:], low),
            pltpu.VMEM((n,) + rows_half[2:], low),
            pltpu.VMEM((2, n, length // n, width), low),
            pltpu.VMEM((n, 2, 2, rows_half[2], (count + 1) // 2 * wide), low),
            pltpu.VMEM((n, 2, rows_half[2], (count + 1) // 2 * wide), low),
            pltpu.VMEM((n, 2, rows_half[2], (count + 1) // 2 * wide), low),
            pltpu.VMEM((rows_half[2], n * rows_half[3]), low),
            pltpu.VMEM((rows_half[2], n * rows_half[3]), low),
            pltpu.VMEM(cols_half[1:], low),
            pltpu.VMEM((n,) + out_half[2:], low),
            pltpu.VMEM((rows, width), low),
            pltpu.VMEM(low_heads.shape, low),
            pltpu.VMEM(log_sums.shape, f32),
            pltpu.VMEM(lin.shape, f32),
            pltpu.VMEM(cosine.shape, f32),
            pltpu.VMEM(sine.shape, f32),
        ]
        + [
            pltpu.SemaphoreType.DMA((group, n)),
            pltpu.SemaphoreType.DMA((group, n)),
            pltpu.SemaphoreType.DMA((count, n)),
            pltpu.SemaphoreType.DMA((count, n)),
            pltpu.SemaphoreType.DMA((4,)),
            pltpu.SemaphoreType.DMA((10,)),
            pltpu.SemaphoreType.DMA((6,)),
            pltpu.SemaphoreType.DMA((6,)),
            pltpu.SemaphoreType.DMA((2, n)),
            pltpu.SemaphoreType.DMA((2, n)),
            pltpu.SemaphoreType.DMA((5,)),
            pltpu.SemaphoreType.DMA((5,)),
        ],
        compiler_params=pltpu.CompilerParams(
            collective_id=3, has_side_effects=True, vmem_limit_bytes=VMEM_BYTES
        ),
        cost_estimate=pl.CostEstimate(
            flops=40 * group * length * length * wide, bytes_accessed=2**26, transcendentals=0
        ),
    )(low_heads, log_sums, lin, cosine, sine, gain, *above, w_output, *feed_terms, normed)


def last_kernel(n, widths, x_ref, norm_ref, f_gain, h_gain, q_sum, w_ref, b_ref, o_ref, *refs):
    g_ref, u_ref, d_ref, y_ref = refs[:4]
    dx_out, n_out, y_out, q_all, o_all, g_all, u_all, d_all = refs[4:12]
    q1, q3, q4, q5, n1, n2, n3, n4, o3, o4, blocks, flat, w_all, y_own, y_all = refs[12:27]
    load_sem, x_send, x_recv, a_send, a_recv, own_sem, y_send, y_recv = refs[27:35]
    f_send, f_recv, f_own, o_send, o_recv, o_own, q_send, q_recv, q_own = refs[35:]
    f32, low = jnp.float32, jnp.bfloat16
    me = lax.axis_index("ctx")
    others = [lax.rem(me + hop, n) for hop in range(1, n)]
    mine_x = lax.div(lax.axis_index("rep"), 2)
    core, across = rep_partners()
    loads = (
        pltpu.make_async_copy(q_sum.at[:, mine_x], q1, load_sem.at[0]),
        pltpu.make_async_copy(b_ref, blocks, load_sem.at[1]),
        pltpu.make_async_copy(w_ref, w_all, load_sem.at[2]),
    )
    y_load = pltpu.make_async_copy(y_ref, y_own, load_sem.at[3])
    y_load.start()
    for copy in loads:
        copy.start()
    place = ring_place(me, n)
    toward = (around(place, 1, n), around(place, -1, n))
    y_half = y_own.shape[1] // 2
    y_parts = (pl.ds(0, y_half), pl.ds(y_half, y_half))

    def y_copy(step, side):
        source = y_own if step == 0 else y_all
        return remote(
            source.at[step, y_parts[side]],
            y_all.at[step + 1, y_parts[side]],
            y_send.at[side, step + 1],
            y_recv.at[side, step + 1],
            toward[side],
        )

    def y_hop(step):
        if step > 0:
            for side in (0, 1):
                y_copy(step - 1, side).wait_recv()
            summed = y_all[step].astype(f32) + y_own[step].astype(f32)
            (y_out if step == n - 1 else y_all.at[step])[...] = summed.astype(low)
        if step < n - 1:
            for side in (0, 1):
                y_copy(step, side).start()

    def cross(at, source, target, other):
        return remote(source, target, x_send.at[at], x_recv.at[at], other, "rep")

    steps = (
        cross(0, q_sum.at[:, 1 - mine_x], q3, across),
        cross(1, n1, n2, core),
        cross(2, n2, n3, across),
    )

    def swap_out(at, hop):
        source, target = ((o_ref, o3), (q3, q4), (n3, n4))[at]
        other = others[hop - 1]
        return remote(
            source if at == 2 else source.at[other],
            target.at[me],
            a_send.at[at, hop],
            a_recv.at[at, hop],
            other,
        )

    def swap_own(at):
        source, target = ((o_ref, o3), (q3, q4), (n3, n4))[at]
        return pltpu.make_async_copy(
            source if at == 2 else source.at[me], target.at[me], own_sem.at[at]
        )

    def swap_all(at):
        swap_own(at).start()
        for hop in range(1, n):
            swap_out(at, hop).start()

    def swapped(at):
        swap_own(at).wait()
        for hop in range(1, n):
            swap_out(at, hop).wait()

    few = o4.shape[0]
    quarter = d_ref.shape[1]

    def rows_of(target):
        return lambda r: target.at[pl.ds(pl.multiple_of(r * few, 16), few)]

    feed = RepShare(
        [
            (g_ref, rows_of(g_all)),
            (u_ref, rows_of(u_all)),
            (d_ref, lambda r: d_all.at[:, pl.ds(pl.multiple_of(r * quarter, quarter), quarter)]),
        ],
        f_send,
        f_recv,
        f_own,
    )
    last_q = RepShare([(q5, rows_of(q_all))], q_send, q_recv, q_own)
    last_o = RepShare([(o4, rows_of(o_all))], o_send, o_recv, o_own)

    greet(others, rep_partners())
    steps[0].start()
    feed.begin()
    y_load.wait()
    y_hop(0)
    swap_all(0)
    for copy in loads:
        copy.wait()
    side_by_side(blocks, flat)
    rows, width = x_ref.shape
    tile = 256

    @pl.loop(0, width // tile)
    def _(at):
        cols = pl.ds(pl.multiple_of(at * tile, tile), tile)
        dx_out[:, cols] = product_back(flat[...], w_rows(w_all, at, tile))

    y_hop(1)
    steps[0].wait()

    @pl.loop(0, n)
    def _(owner):
        q3[owner] = (q3[owner].astype(f32) + q1[owner].astype(f32)).astype(low)

    swap_all(1)
    y_hop(2)
    n1[...] = jnp.zeros_like(n1)
    chunk = 64
    totals = jnp.zeros((1, width), f32)
    for at in range(rows // chunk):
        here = pl.ds(at * chunk, chunk)
        x = x_ref[here].astype(f32)
        back, terms = norm_back(dx_out[here], x, norm_ref[...])
        totals += jnp.sum(terms, axis=0, keepdims=True)
        dx_out[here] = back
    lanes = n1.shape[1]
    lines = width // lanes
    for at in range(lines):
        here = slice(at * lanes, (at + 1) * lanes)
        n1[at : at + 1] = totals[:, here]
        n1[lines + at : lines + at + 1] = f_gain[:, here]
    heads = h_gain[0:2]
    heads = heads + pltpu.roll(heads, lanes // 2, 1)
    n1[2 * lines : 2 * lines + 1] = pack(heads[0:1], heads[1:2])
    steps[1].start()
    y_hop(3)
    steps[1].wait()
    n2[...] += n1[...]
    steps[2].start()
    feed.middle(0)
    y_hop(4)
    swapped(1)
    q_wide, k_wide = widths
    for source in range(n):
        at = 0
        place = 0
        for wide in (q_wide, k_wide, k_wide):
            start = place + source * wide
            q5[:, start : start + wide] = q4[source, :, at : at + wide]
            at += wide
            place += n * wide
    last_q.begin()
    y_hop(5)
    feed.middle(1)
    swapped(0)

    @pl.loop(0, few // 16)
    def _(at):
        here = pl.ds(pl.multiple_of(at * 16, 16), 16)
        total = o3[0, here].astype(f32)
        for source in range(1, n):
            total += o3[source, here].astype(f32)
        o4[here] = total.astype(low)

    last_o.begin()
    y_hop(6)
    steps[2].wait()
    n3[...] += n2[...]
    swap_all(2)
    feed.middle(2)
    last_q.middle()
    last_o.middle()
    for step in range(7, n):
        y_hop(step)
    swapped(2)
    total = n4[0]
    for source in range(1, n):
        total += n4[source]
    n_out[...] = total
    feed.end()
    last_q.end()
    last_o.end()
    for step in range(n - 1):
        for side in (0, 1):
            y_copy(step, side).wait_send()


def w_rows(w_all, at, tile):
    n, reps, few, cols = w_all.shape
    rows = [w_all[lax.div(at * tile + start, reps * few), lax.rem(lax.div(at * tile + start, few), reps),
                  pl.ds(pl.multiple_of(lax.rem(at * tile + start, few), 16), 16)]
            for start in range(0, tile, 16)]
    return jnp.concatenate(rows, axis=0)


def last_sums(x, norm_gain, ffn_terms, head_terms, q_sum, w_full, blocks, parts, widths):
    o_part, g_part, u_part, d_part, y_part = parts
    n = lax.axis_size("ctx")
    reps = lax.axis_size("rep")
    f32, low = jnp.float32, jnp.bfloat16
    few, wide = q_sum.shape[2:]
    rows, width = x.shape
    shard = reps * few
    out_wide = o_part.shape[2]
    feed_wide = g_part.shape[1]
    lines = -(-(2 * width // 128 + 1) // 8) * 8
    return pl.pallas_call(
        functools.partial(last_kernel, n, widths),
        out_shape=[
            jax.ShapeDtypeStruct((rows, width), f32),
            jax.ShapeDtypeStruct((lines, 128), f32),
            jax.ShapeDtypeStruct(y_part.shape[1:], low),
            jax.ShapeDtypeStruct((shard, w_full.shape[3]), low),
            jax.ShapeDtypeStruct((shard, out_wide), low),
            jax.ShapeDtypeStruct((shard, feed_wide), low),
            jax.ShapeDtypeStruct((shard, feed_wide), low),
            jax.ShapeDtypeStruct((d_part.shape[0], reps * d_part.shape[1]), low),
        ],
        in_specs=[VMEM] * 4 + [ANY] * 8,
        out_specs=[VMEM] * 3 + [ANY] * 5,
        scratch_shapes=[
            pltpu.VMEM((n, few, wide), low),
            pltpu.VMEM((n, few, wide), low),
            pltpu.VMEM((n, few, wide), low),
            pltpu.VMEM((few, w_full.shape[3]), low),
            pltpu.VMEM((lines, 128), f32),
            pltpu.VMEM((lines, 128), f32),
            pltpu.VMEM((lines, 128), f32),
            pltpu.VMEM((n, lines, 128), f32),
            pltpu.VMEM((n, few, out_wide), low),
            pltpu.VMEM((few, out_wide), low),
            pltpu.VMEM(blocks.shape, low),
            pltpu.VMEM((rows, w_full.shape[3]), low),
            pltpu.VMEM(w_full.shape, low),
            pltpu.VMEM(y_part.shape, low),
            pltpu.VMEM(y_part.shape, low),
            pltpu.SemaphoreType.DMA((4,)),
            pltpu.SemaphoreType.DMA((3,)),
            pltpu.SemaphoreType.DMA((3,)),
            pltpu.SemaphoreType.DMA((3, n)),
            pltpu.SemaphoreType.DMA((3, n)),
            pltpu.SemaphoreType.DMA((3,)),
            pltpu.SemaphoreType.DMA((2, n)),
            pltpu.SemaphoreType.DMA((2, n)),
        ]
        + [
            pltpu.SemaphoreType.DMA(shape)
            for k in (3, 1, 1)
            for shape in ((k, 3), (k, 3), (k,))
        ],
        compiler_params=pltpu.CompilerParams(
            collective_id=4, has_side_effects=True, vmem_limit_bytes=VMEM_BYTES
        ),
    )(x, norm_gain, ffn_terms, head_terms, q_sum, w_full, blocks, *parts)


def feed_kernel(n, tile, normed_ref, grad_ref, wg_src, wu_src, wd_src, wq_ref, *refs):
    y_out, y_hold, b_out, wq_out, g_keep, g_got, u_keep, u_got, d_keep, d_got = refs[:10]
    h_slots, d_slots, y_slots, b_slots, hid, dgate, dup, dwg, dwu, dwd, stage, d_stage, y_stage = refs[10:23]
    wg_ref, wu_ref, wd_ref = refs[23:26]
    h_send, h_recv, y_send, y_recv, b_send, b_recv, d_sem, own_sem, r_send, r_recv, r_own = refs[26:37]
    keep_sem, c_send, c_recv, dc_send, dc_recv, y_sem = refs[37:]
    f32, low = jnp.float32, jnp.bfloat16
    me = lax.axis_index("ctx")
    place = ring_place(me, n)
    right, left = around(place, 1, n), around(place, -1, n)
    rows, width = normed_ref.shape
    half = rows // 2
    parts = (pl.ds(0, half), pl.ds(half, half))
    toward = (right, left)

    def grad_load(step, side):
        owner = around(place, -1 - step if side == 0 else 1 + step, n)
        return pltpu.make_async_copy(
            grad_ref.at[owner, parts[side]],
            d_slots.at[lax.rem(step, 2), parts[side]],
            d_sem.at[lax.rem(step, 2), side],
        )

    def pass_on(step, side):
        return remote(
            h_slots.at[step, parts[side]],
            h_slots.at[step + 1, parts[side]],
            h_send.at[side, step + 1],
            h_recv.at[side, step + 1],
            toward[side],
        )

    def sum_on(slots, send, recv, step, side):
        return remote(
            slots.at[step, parts[side]],
            slots.at[step + 1, parts[side]],
            send.at[side, step + 1],
            recv.at[side, step + 1],
            toward[side],
        )

    def first(side):
        return remote(
            normed_ref.at[parts[side]],
            h_slots.at[0, parts[side]],
            h_send.at[side, 0],
            h_recv.at[side, 0],
            toward[side],
        )

    weight_loads = [
        pltpu.make_async_copy(source, target, own_sem.at[5 + at])
        for at, (source, target) in enumerate(
            ((wg_src, wg_ref), (wu_src, wu_ref), (wd_src, wd_ref))
        )
    ]
    for copy in weight_loads:
        copy.start()
    for side in (0, 1):
        grad_load(0, side).start()
    keep = pltpu.make_async_copy(normed_ref, h_slots.at[n - 1], own_sem.at[0])
    keep.start()
    share = RepShare([(wq_ref, lambda r: wq_out.at[:, r])], r_send, r_recv, r_own)
    greet((left, right), rep_partners())
    for side in (0, 1):
        first(side).start()
    share.begin()
    y_slots[0] = jnp.zeros(y_slots.shape[1:], low)
    b_slots[0] = jnp.zeros((rows, width), low)

    @pl.loop(0, width // tile)
    def _(at):
        cols = pl.ds(pl.multiple_of(at * tile, tile), tile)
        dwg[cols, :] = jnp.zeros((tile, dwg.shape[1]), f32)
        dwu[cols, :] = jnp.zeros((tile, dwu.shape[1]), f32)
        dwd[:, cols] = jnp.zeros((dwd.shape[0], tile), f32)

    keep.wait()
    for copy in weight_loads:
        copy.wait()

    def next_block(step):
        for side in (0, 1):
            block = h_slots.at[step, parts[side]]
            remote(block, block, h_send.at[side, step], h_recv.at[side, step], right).wait_recv()

            @pl.when(step < n - 2)
            def _():
                pass_on(step, side).start()

    def hold(step):
        turn = lax.rem(step, 2)
        return pltpu.make_async_copy(y_stage.at[turn], y_hold.at[step], y_sem.at[turn])

    next_block(0)
    kept = y_slots.shape[2] // tile

    @pl.loop(0, n)
    def _(step):
        @pl.when(step < n - 1)
        def _():
            for side in (0, 1):
                grad_load(step + 1, side).start()

        for side in (0, 1):
            grad_load(step, side).wait()

        @pl.when(step == n // 2)
        def _():
            share.middle()

        turn = lax.rem(step, 2)
        h = h_slots[step]
        gate = jnp.dot(h, wg_ref[...], preferred_element_type=f32)
        up = jnp.dot(h, wu_ref[...], preferred_element_type=f32)
        grad_hidden = product_back(d_slots[turn], wd_ref[...])
        sigma = jax.nn.sigmoid(gate)
        silu = gate * sigma
        hid[...] = (silu * up).astype(low)
        dup[...] = (grad_hidden * silu).astype(low)
        dgate[...] = (grad_hidden * up * sigma * (1.0 + gate * (1.0 - sigma))).astype(low)

        @pl.when(step < n - 2)
        def _():
            next_block(step + 1)

        @pl.when(step > 0)
        def _():
            for side in (0, 1):
                sum_on(b_slots, b_send, b_recv, step - 1, side).wait_recv()

        @pl.loop(0, width // tile)
        def _(at):
            cols = pl.ds(pl.multiple_of(at * tile, tile), tile)
            back = product_back(dgate[...], wg_ref[cols, :]) + product_back(
                dup[...], wu_ref[cols, :]
            )
            b_slots[step, :, cols] = (b_slots[step, :, cols].astype(f32) + back).astype(low)

        @pl.when(step < n - 1)
        def _():
            for side in (0, 1):
                sum_on(b_slots, b_send, b_recv, step, side).start()

        @pl.when(step > 0)
        def _():
            for side in (0, 1):
                sum_on(y_slots, y_send, y_recv, step - 1, side).wait_recv()

        @pl.loop(0, kept)
        def _(at):
            cols = pl.ds(pl.multiple_of(at * tile, tile), tile)
            added = jnp.dot(hid[...], wd_ref[:, cols], preferred_element_type=f32)
            y_slots[step, :, cols] = (y_slots[step, :, cols].astype(f32) + added).astype(low)

        @pl.when(step < n - 1)
        def _():
            for side in (0, 1):
                sum_on(y_slots, y_send, y_recv, step, side).start()

        @pl.when(step >= 2)
        def _():
            hold(step - 2).wait()

        @pl.loop(kept, width // tile)
        def _(at):
            cols = pl.ds(pl.multiple_of(at * tile, tile), tile)
            there = pl.ds(pl.multiple_of((at - kept) * tile, tile), tile)
            added = jnp.dot(hid[...], wd_ref[:, cols], preferred_element_type=f32)
            y_stage[turn, :, there] = added.astype(low)

        hold(step).start()

        @pl.loop(0, width // tile)
        def _(at):
            cols = pl.ds(pl.multiple_of(at * tile, tile), tile)
            h_cols = h_slots[step, :, cols]
            dwg[cols, :] += product_rows(h_cols, dgate[...])
            dwu[cols, :] += product_rows(h_cols, dup[...])
            dwd[:, cols] += product_rows(hid[...], d_slots[turn, :, cols])

    outs = (
        pltpu.make_async_copy(y_slots.at[n - 1], y_out, own_sem.at[1]),
        pltpu.make_async_copy(b_slots.at[n - 1], b_out, own_sem.at[2]),
    )
    for copy in outs:
        copy.start()
    hold(n - 2).wait()
    hold(n - 1).wait()
    core, _ = rep_partners()
    mine = lax.rem(lax.axis_index("rep"), 2)
    wide = width // 4
    few = g_keep.shape[2]

    def column_copies(side):
        quarter = (2 * side + mine, 2 * side + 1 - mine)
        return quarter, (
            pltpu.make_async_copy(d_stage.at[2 * side], d_keep.at[side], own_sem.at[3 + side]),
            remote(
                d_stage.at[2 * side + 1],
                d_got.at[side],
                dc_send.at[side],
                dc_recv.at[side],
                core,
                "rep",
            ),
        )

    for side in (0, 1):
        quarters, copies = column_copies(side)
        for at, (quarter, copy) in enumerate(zip(quarters, copies)):
            cols = pl.ds(pl.multiple_of(quarter * wide, wide), wide)
            d_stage[2 * side + at] = dwd[:, cols].astype(low)
            copy.start()

    def row_copies(owner, turn):
        for at, (total, keep, got) in enumerate(((dwg, g_keep, g_got), (dwu, u_keep, u_got))):
            for side in (0, 1):
                slot = 4 * at + 2 * side
                yield total, slot, 2 * side + mine, pltpu.make_async_copy(
                    stage.at[turn, slot], keep.at[owner, side], keep_sem.at[turn, slot // 2]
                )
                yield total, slot + 1, 2 * side + 1 - mine, remote(
                    stage.at[turn, slot + 1],
                    got.at[owner, side],
                    c_send.at[owner, slot // 2],
                    c_recv.at[owner, slot // 2],
                    core,
                    "rep",
                )

    def row_wait(owner, turn):
        for _, slot, _, copy in row_copies(owner, turn):
            if slot % 2 == 0:
                copy.wait()
            else:
                copy.wait_send()

    @pl.loop(0, n)
    def _(owner):
        turn = lax.rem(owner, 2)

        @pl.when(owner >= 2)
        def _():
            row_wait(owner - 2, turn)

        for total, slot, quarter, copy in row_copies(owner, turn):
            start = pl.multiple_of((4 * owner + quarter) * few, 8)
            stage[turn, slot] = total[pl.ds(start, few), :].astype(low)
            copy.start()

    for owner in (n - 2, n - 1):
        row_wait(owner, owner % 2)

    @pl.loop(0, n)
    def _(owner):
        for _, slot, _, copy in row_copies(owner, 0):
            if slot % 2 == 1:
                copy.wait_recv()

    for side in (0, 1):
        for copy in column_copies(side)[1]:
            copy.wait()
    for copy in outs:
        copy.wait()
    share.end()
    for side in (0, 1):
        first(side).wait_send()

        @pl.loop(0, n - 2)
        def _(step):
            pass_on(step, side).wait_send()

        @pl.loop(0, n - 1)
        def _(step):
            sum_on(b_slots, b_send, b_recv, step, side).wait_send()
            sum_on(y_slots, y_send, y_recv, step, side).wait_send()


def feed_scratch(n, rows, width, cols):
    low = jnp.bfloat16
    return [
        pltpu.VMEM((n, rows, width), low),
        pltpu.VMEM((2, rows, width), low),
        pltpu.VMEM((n, rows, width // 2), low),
        pltpu.VMEM((n, rows, width), low),
        pltpu.VMEM((rows, cols), low),
        pltpu.VMEM((rows, cols), low),
        pltpu.VMEM((rows, cols), low),
        pltpu.VMEM((width, cols), jnp.float32),
        pltpu.VMEM((width, cols), jnp.float32),
        pltpu.VMEM((cols, width), jnp.float32),
        pltpu.VMEM((2, 8, width // (4 * n), cols), low),
        pltpu.VMEM((4, cols, width // 4), low),
        pltpu.VMEM((2, rows, width // 2), low),
        pltpu.VMEM((width, cols), low),
        pltpu.VMEM((width, cols), low),
        pltpu.VMEM((cols, width), low),
    ]


def feed_fits(n, rows, width, cols):
    wide = -(-cols // 128) * 128
    slots = (3 * n + 2) * rows * width * 2 + 3 * rows * wide * 2
    weights = 3 * width * wide * (2 + 4) + 4 * width * wide * 2 // n + width * wide * 2
    return slots + weights + 24 * rows * wide <= VMEM_BYTES


def feed_ring(normed, grad_all, w_gate, w_up, w_down, quarter):
    n = lax.axis_size("ctx")
    rows, width = normed.shape
    cols = w_gate.shape[1]
    low = jnp.bfloat16
    reps = lax.axis_size("rep")
    return pl.pallas_call(
        functools.partial(feed_kernel, n, 256),
        out_shape=[
            jax.ShapeDtypeStruct((rows, width // 2), low),
            jax.ShapeDtypeStruct((n, rows, width // 2), low),
            jax.ShapeDtypeStruct((rows, width), low),
            jax.ShapeDtypeStruct((n, reps) + quarter.shape[1:], quarter.dtype),
        ]
        + [jax.ShapeDtypeStruct((n, 2, width // (4 * n), cols), low)] * 4
        + [jax.ShapeDtypeStruct((2, cols, width // 4), low)] * 2,
        in_specs=[ANY] * 6,
        out_specs=[ANY] * 10,
        scratch_shapes=feed_scratch(n, rows, width, cols)
        + [pltpu.SemaphoreType.DMA((2, n))] * 6
        + [pltpu.SemaphoreType.DMA((2, 2)), pltpu.SemaphoreType.DMA((8,))]
        + [pltpu.SemaphoreType.DMA((1, 3))] * 2
        + [pltpu.SemaphoreType.DMA((1,))]
        + [pltpu.SemaphoreType.DMA((2, 4))]
        + [pltpu.SemaphoreType.DMA((n, 4))] * 2
        + [pltpu.SemaphoreType.DMA((2,))] * 3,
        compiler_params=pltpu.CompilerParams(
            collective_id=1, has_side_effects=True, vmem_limit_bytes=VMEM_BYTES
        ),
        cost_estimate=pl.CostEstimate(
            flops=18 * n * rows * width * cols, bytes_accessed=40 * width * cols, transcendentals=0
        ),
    )(normed, grad_all, w_gate, w_up, w_down, quarter)


def columns_by_owner(shard, parts):
    rows, width = shard.shape
    return shard.reshape(rows, parts, width // parts).transpose(1, 0, 2)


def columns_joined(blocks):
    parts, rows, width = blocks.shape
    return blocks.transpose(1, 0, 2).reshape(rows, parts * width)


def take_gains(gains, width):
    gains = gains.astype(jnp.float32)
    return gains[:width, 0], gains[:width, 1], gains[width:, 0], gains[width:, 1]


class HeadAttention:
    def __init__(self, dims, shards, feed_shards, w_down, gains_shard, tokens, cotangent):
        self.dims = dims
        parts, seqs, span, width, head_dim, heads, kv_heads = dims
        low = jnp.bfloat16
        group = heads // kv_heads
        self.group = group
        rows = seqs * span
        length = parts * span
        few = gains_shard.shape[0]
        padded = jnp.pad(gains_shard.astype(low).astype(jnp.float32).T, ((0, 6), (0, -few % 128)))
        (
            self.normed,
            self.lin,
            gains_all,
            out_quarter,
            self.quarter,
            w_gate,
            w_up,
            self.w_down,
        ) = enter(tokens.reshape(rows, width), padded, shards, feed_shards, w_down, head_dim)
        gains = gains_all[:, :2, :few].transpose(0, 2, 1).reshape(-1, 2)
        self.gain_attn, self.gain_ffn, gain_query, gain_key = take_gains(gains, width)
        self.cosine, self.sine = (
            jnp.asarray(table) for table in rotary_constants(length, head_dim, seqs)
        )
        self.gain = jnp.pad(
            jnp.stack([jnp.concatenate([g] * seqs) for g in (gain_query, gain_key)]), ((0, 6), (0, 0))
        )
        self.tokens = tokens.reshape(rows, width)
        (
            self.low_heads,
            self.log_sums,
            self.attended,
            self.resid,
            self.normed_two,
            self.grad_all,
            w_output,
        ) = attend(
            self.lin,
            self.cosine,
            self.sine,
            self.gain,
            self.tokens,
            self.gain_ffn[None],
            cotangent.reshape(rows, width),
            out_quarter,
        )
        self.w_output = w_output.reshape(width, -1)
        self.w_gate = w_gate.reshape(width, -1)
        self.w_up = w_up.reshape(width, -1)

    def feed(self):
        self.added, self.held, back, self.w_full, *self.feed_terms = feed_ring(
            self.normed_two, self.grad_all, self.w_gate, self.w_up, self.w_down, self.quarter
        )
        return back

    def backward(self, normed_two_grad, grad_low):
        span, width = self.dims[2:4]
        self.blocks, self.q_sum, self.head_terms, *parts_done, grad_resid, ffn_terms = attend_back(
            self.low_heads,
            self.log_sums,
            self.lin,
            self.cosine,
            self.sine,
            self.gain,
            (normed_two_grad, self.resid, grad_low, self.gain_ffn[None], self.attended),
            self.w_output.reshape(-1, span, width),
            self.feed_terms,
            self.normed,
        )
        self.parts_done = parts_done
        return grad_resid, ffn_terms[0]

    def finish(self, grad_resid, ffn_terms):
        parts, seqs, span, width, head_dim, heads, kv_heads = self.dims
        gate, up, down, out = self.parts_done
        back, gains, added, mixed, out, gate, up, down = last_sums(
            self.tokens,
            self.gain_attn[None],
            ffn_terms[None],
            self.head_terms,
            self.q_sum,
            self.w_full,
            self.blocks,
            (out, gate, up, down, self.held),
            (self.group * head_dim, head_dim),
        )
        gains = gains.reshape(-1)
        one, two = gains[:width], gains[width : 2 * width]
        query = gains[2 * width : 2 * width + head_dim]
        key = gains[2 * width + head_dim : 2 * width + 2 * head_dim]
        gains = jnp.stack([jnp.concatenate([one, query]), jnp.concatenate([two, key])], axis=1)
        count = gains.shape[0] // parts
        gains = lax.dynamic_slice_in_dim(gains, lax.axis_index("ctx") * count, count, 0)
        cuts = (heads * head_dim, (heads + kv_heads) * head_dim)
        grads = (
            mixed[:, : cuts[0]], mixed[:, cuts[0] : cuts[1]], mixed[:, cuts[1] :], out, gate, up, down, gains
        )
        added = jnp.concatenate([self.added, added], axis=1).astype(jnp.float32)
        return grad_resid + back, self.resid + added, grads


class RowAttention:
    def __init__(self, dims, shards, feed_shards, w_down, gains_shard, tokens, cotangent):
        self.dims = dims
        parts, seqs, span, width, head_dim, heads, kv_heads = dims
        low = jnp.bfloat16
        gains = lax.all_gather(gains_shard.astype(low), "ctx", axis=0, tiled=True)
        self.gain_attn, self.gain_ffn, self.gain_query, self.gain_key = take_gains(gains, width)
        place = lax.axis_index("ctx")
        rows = seqs * span
        self.group = heads // kv_heads
        self.weights = tuple(
            lax.all_gather(w.astype(low), "ctx", axis=0, tiled=True) for w in shards[:3]
        )
        self.w_output = lax.all_gather(shards[3].astype(low), "ctx", axis=0, tiled=True)
        self.w_gate, self.w_up = (
            swap(columns_by_owner(w.astype(low), parts)).reshape(width, -1) for w in feed_shards
        )
        self.w_down = w_down.astype(low)
        self.grad_all = gather(cotangent.reshape(rows, width))
        inputs = tokens.astype(jnp.float32).reshape(rows, width)
        self.normed = (inputs * rms_scale(inputs) * self.gain_attn).astype(jnp.bfloat16)
        query_lin, key_lin, value_lin = (product(self.normed, w) for w in self.weights)
        self.cosine, self.sine = rotary_tables(place * span, span, head_dim)
        self.query_heads = query_lin.reshape(seqs, span, heads, head_dim)
        query_low = rotate(
            self.query_heads * rms_scale(self.query_heads) * self.gain_query, self.cosine, self.sine
        ).astype(jnp.bfloat16)
        self.key_heads = key_lin.reshape(seqs, span, kv_heads, head_dim)
        key_low = rotate(
            self.key_heads * rms_scale(self.key_heads) * self.gain_key, self.cosine, self.sine
        ).astype(jnp.bfloat16)
        kv_width = kv_heads * head_dim
        self.keys_all = lax.all_gather(
            key_low.reshape(seqs, span, kv_width), "ctx", axis=1, tiled=True
        )
        self.values_all = lax.all_gather(
            value_lin.astype(jnp.bfloat16).reshape(seqs, span, kv_width), "ctx", axis=1, tiled=True
        )
        self.query_grouped = query_low.reshape(seqs, span, kv_heads, self.group, head_dim)
        query_pos = place * span + jnp.arange(span)
        self.visible = jnp.arange(parts * span)[None, :] <= query_pos[:, None]
        self.attended = self.forward()
        self.resid = inputs + product(self.attended, self.w_output)
        normed_two = self.resid * rms_scale(self.resid) * self.gain_ffn
        self.normed_two = normed_two.astype(jnp.bfloat16)
        self.tokens = inputs

    def feed(self):
        self.added, back, *self.feed_terms = feed_plain(
            self.normed_two, self.grad_all, self.w_gate, self.w_up, self.w_down
        )
        return back

    def head_scores(self, index):
        head_dim = self.dims[4]
        query_group = lax.dynamic_index_in_dim(self.query_grouped, index, 2, keepdims=False)
        key_group = lax.dynamic_slice_in_dim(self.keys_all, index * head_dim, head_dim, 2)
        value_group = lax.dynamic_slice_in_dim(self.values_all, index * head_dim, head_dim, 2)
        raw = (
            jnp.einsum("scjd,skd->sjck", query_group, key_group, preferred_element_type=jnp.float32)
            * score_scale
        )
        return (query_group, key_group, value_group, jnp.where(self.visible, raw, -1e30))

    def forward(self):
        parts, seqs, span, width, head_dim, heads, kv_heads = self.dims

        def forward_head(index, carry):
            attended, log_sums = carry
            _, _, value_group, scores = self.head_scores(index)
            top = jnp.max(scores, axis=-1, keepdims=True)
            expo = jnp.exp(scores - top)
            total = jnp.sum(expo, axis=-1, keepdims=True)
            probs = (expo / total).astype(jnp.bfloat16)
            head_out = jnp.einsum(
                "sjck,skd->scjd", probs, value_group, preferred_element_type=jnp.float32
            )
            attended = lax.dynamic_update_index_in_dim(attended, head_out, index, 2)
            log_sums = lax.dynamic_update_index_in_dim(
                log_sums, (top + jnp.log(total))[..., 0], index, 0
            )
            return (attended, log_sums)

        attended, self.log_sums = lax.fori_loop(
            0,
            kv_heads,
            forward_head,
            (
                jnp.zeros((seqs, span, kv_heads, self.group, head_dim), jnp.float32),
                jnp.zeros((kv_heads, seqs, self.group, span), jnp.float32),
            ),
        )
        return attended.reshape(seqs * span, heads * head_dim).astype(jnp.bfloat16)

    def backward(self, normed_two_grad, grad_low):
        back_two, ffn_terms = norm_back(
            normed_two_grad.astype(jnp.float32), self.resid, self.gain_ffn
        )
        grad_resid = grad_low.astype(jnp.float32) + back_two
        resid_low = grad_resid.astype(jnp.bfloat16)
        self.out_term = product_rows(self.attended, resid_low)
        self.heads_backward(product_back(resid_low, self.w_output).astype(jnp.bfloat16))
        return grad_resid, jnp.sum(ffn_terms, axis=0)

    def heads_backward(self, grad_rows):
        parts, seqs, span, width, head_dim, heads, kv_heads = self.dims
        group = self.group
        rows = seqs * span
        length = parts * span
        kv_width = kv_heads * head_dim
        grad_grouped = grad_rows.reshape(seqs, span, kv_heads, group, head_dim)

        def backward_head(index, carry):
            query_acc, key_acc, value_acc = carry
            query_group, key_group, value_group, scores = self.head_scores(index)
            log_group = lax.dynamic_index_in_dim(self.log_sums, index, 0, keepdims=False)
            probs = jnp.exp(scores - log_group[..., None])
            grad_group = lax.dynamic_index_in_dim(grad_grouped, index, 2, keepdims=False)
            grad_probs = jnp.einsum(
                "scjd,skd->sjck", grad_group, value_group, preferred_element_type=jnp.float32
            )
            inner = jnp.sum(probs * grad_probs, axis=-1, keepdims=True)
            grad_scores = (probs * (grad_probs - inner)).astype(jnp.bfloat16)
            grad_query = (
                jnp.einsum(
                    "sjck,skd->scjd", grad_scores, key_group, preferred_element_type=jnp.float32
                )
                * score_scale
            )
            grad_key = (
                jnp.einsum(
                    "sjck,scjd->skd", grad_scores, query_group, preferred_element_type=jnp.float32
                )
                * score_scale
            )
            grad_value = jnp.einsum(
                "sjck,scjd->skd",
                probs.astype(jnp.bfloat16),
                grad_group,
                preferred_element_type=jnp.float32,
            )
            query_acc = lax.dynamic_update_index_in_dim(query_acc, grad_query, index, 2)
            key_acc = lax.dynamic_update_slice_in_dim(key_acc, grad_key, index * head_dim, 2)
            value_acc = lax.dynamic_update_slice_in_dim(value_acc, grad_value, index * head_dim, 2)
            return (query_acc, key_acc, value_acc)

        query_acc, key_acc, value_acc = lax.fori_loop(
            0,
            kv_heads,
            backward_head,
            (
                jnp.zeros((seqs, span, kv_heads, group, head_dim), jnp.float32),
                jnp.zeros((seqs, length, kv_width), jnp.float32),
                jnp.zeros((seqs, length, kv_width), jnp.float32),
            ),
        )
        key_back, value_back = (
            lax.psum_scatter(
                acc.astype(jnp.bfloat16), "ctx", scatter_dimension=1, tiled=True
            ).astype(jnp.float32)
            for acc in (key_acc, value_acc)
        )
        query_rot = rotate_back(
            query_acc.reshape(seqs, span, heads, head_dim), self.cosine, self.sine
        )
        query_back, query_gain_terms = norm_back(query_rot, self.query_heads, self.gain_query)
        key_rot = rotate_back(
            key_back.reshape(seqs, span, kv_heads, head_dim), self.cosine, self.sine
        )
        key_grad, key_gain_terms = norm_back(key_rot, self.key_heads, self.gain_key)
        lows = (
            query_back.reshape(rows, heads * head_dim).astype(jnp.bfloat16),
            key_grad.reshape(rows, kv_width).astype(jnp.bfloat16),
            value_back.reshape(rows, kv_width).astype(jnp.bfloat16),
        )
        normed_grad = sum(product_back(g, w) for g, w in zip(lows, self.weights))
        self.grads = tuple(
            rep_sum(
                lax.psum_scatter(
                    product_rows(self.normed, g).astype(jnp.bfloat16),
                    "ctx",
                    scatter_dimension=0,
                    tiled=True,
                )
            )
            for g in lows
        )
        gain_terms = (
            jnp.sum(query_gain_terms, axis=(0, 1, 2)),
            jnp.sum(key_gain_terms, axis=(0, 1, 2)),
        )
        self.normed_grad, self.gain_terms = normed_grad, gain_terms

    def finish(self, grad_resid, ffn_terms):
        back_one, attn_terms = norm_back(self.normed_grad, self.tokens, self.gain_attn)
        query_gain, key_gain = self.gain_terms
        column_one = jnp.concatenate([jnp.sum(attn_terms, axis=0), query_gain])
        column_two = jnp.concatenate([ffn_terms, key_gain])
        grads = self.weight_grads(jnp.stack([column_one, column_two], axis=1))
        return grad_resid + back_one, self.resid + self.added.astype(jnp.float32), grads

    def weight_grads(self, gains_term):
        parts = self.dims[0]
        reps = lax.axis_size("rep")
        shard = self.dims[3] // parts
        out = swap(rep_scatter(owner_blocks(self.out_term, parts, reps)))
        out = jnp.sum(out.astype(jnp.float32), axis=0).astype(jnp.bfloat16)
        gate, up, down = self.feed_terms
        gate, up = (
            rep_gather(columns_joined(swap(rep_scatter(owner_blocks(term, parts, reps)))))
            for term in (gate, up)
        )
        down = rep_gather(rep_scatter(down.reshape(reps, -1, down.shape[1])))
        gains = rep_sum(lax.psum_scatter(gains_term, "ctx", scatter_dimension=0, tiled=True))
        return self.grads + (
            rep_gather(out).reshape(shard, -1),
            gate.reshape(shard, -1),
            up.reshape(shard, -1),
            down.reshape(-1, down.shape[2]),
            gains,
        )


def feed_plain(normed, grad_all, w_gate, w_up, w_down):
    low = jnp.bfloat16
    rows, width = normed.shape
    parts = lax.axis_size("ctx")
    normed_all = gather(normed).reshape(parts * rows, width)
    grad_all = grad_all.reshape(parts * rows, width)
    gate = product(normed_all, w_gate)
    up = product(normed_all, w_up)
    sigma = jax.nn.sigmoid(gate)
    hidden_low = (gate * sigma * up).astype(low)
    added = scatter_sum(product(hidden_low, w_down).astype(low).reshape(parts, rows, width))
    grad_hidden = product_back(grad_all, w_down)
    up_grad_low = (grad_hidden * gate * sigma).astype(low)
    gate_grad_low = (grad_hidden * up * sigma * (1.0 + gate * (1.0 - sigma))).astype(low)
    back = product_back(gate_grad_low, w_gate) + product_back(up_grad_low, w_up)
    return (
        added,
        scatter_sum(back.astype(low).reshape(parts, rows, width)),
        product_rows(normed_all, gate_grad_low),
        product_rows(normed_all, up_grad_low),
        product_rows(hidden_low, grad_all),
    )


def owner_blocks(term, parts, reps):
    rows, cols = term.shape
    return term.reshape(parts, reps, rows // (parts * reps), cols).transpose(1, 0, 2, 3)


def body(

    tokens,
    cotangent,
    query_weight,
    key_weight,
    value_weight,
    output_weight,
    gate_weight,
    up_weight,
    down_weight,
    norm_gains,
    first_query,
    first_key,
    first_value,
    first_output,
    first_gate,
    first_up,
    first_down,
    first_gains,
    second_query,
    second_key,
    second_value,
    second_output,
    second_gate,
    second_up,
    second_down,
    second_gains,
):
    seqs, span, width = tokens.shape
    rows = seqs * span
    head_dim = HD
    heads = query_weight.shape[1] // head_dim
    kv_heads = key_weight.shape[1] // head_dim
    parts = lax.axis_size("ctx")
    dims = (parts, seqs, span, width, head_dim, heads, kv_heads)
    low = jnp.bfloat16
    reps = lax.axis_size("rep")
    packs = parts == kv_heads and reps == 4 and seqs * head_dim == 128
    packs = packs and feed_fits(parts, rows, width, down_weight.shape[0])
    attention = (HeadAttention if packs else RowAttention)(
        dims,
        (query_weight, key_weight, value_weight, output_weight),
        (gate_weight, up_weight),
        down_weight,
        norm_gains,
        tokens,
        cotangent,
    )
    grad_low = cotangent.reshape(rows, width)
    grad_resid, ffn_terms = attention.backward(attention.feed(), grad_low)
    weights = (
        query_weight,
        key_weight,
        value_weight,
        output_weight,
        gate_weight,
        up_weight,
        down_weight,
        norm_gains,
    )
    firsts = (
        first_query,
        first_key,
        first_value,
        first_output,
        first_gate,
        first_up,
        first_down,
        first_gains,
    )
    seconds = (
        second_query,
        second_key,
        second_value,
        second_output,
        second_gate,
        second_up,
        second_down,
        second_gains,
    )
    rates = (0.05, 0.05, 0.05, 0.3, 0.05, 0.05, 0.05, 0.5)
    decays = (0.1, 0.1, 0.1, 0.1, 0.1, 0.1, 0.1, 0.0)
    input_gradient, activations, grads = attention.finish(grad_resid, ffn_terms)
    activations = activations.astype(low).reshape(seqs, span, width)
    input_gradient = input_gradient.reshape(seqs, span, width)
    updated = [
        adamw(w, g.astype(jnp.float32), m, u, rate, decay)
        for w, g, m, u, rate, decay in zip(weights, grads, firsts, seconds, rates, decays)
    ]
    return (
        activations,
        input_gradient,
        updated[0][0],
        updated[1][0],
        updated[2][0],
        updated[3][0],
        updated[4][0],
        updated[5][0],
        updated[6][0],
        updated[7][0],
        updated[0][1],
        updated[1][1],
        updated[2][1],
        updated[3][1],
        updated[4][1],
        updated[5][1],
        updated[6][1],
        updated[7][1],
        updated[0][2],
        updated[1][2],
        updated[2][2],
        updated[3][2],
        updated[4][2],
        updated[5][2],
        updated[6][2],
        updated[7][2],
    )


def solution(mesh):
    placed = (
        P("rep", "ctx", None),
        P("rep", "ctx", None),
        P("ctx", None),
        P("ctx", None),
        P("ctx", None),
        P("ctx", None),
        P("ctx", None),
        P("ctx", None),
        P("ctx", None),
        P("ctx", None),
        P("ctx", None),
        P("ctx", None),
        P("ctx", None),
        P("ctx", None),
        P("ctx", None),
        P("ctx", None),
        P("ctx", None),
        P("ctx", None),
        P("ctx", None),
        P("ctx", None),
        P("ctx", None),
        P("ctx", None),
        P("ctx", None),
        P("ctx", None),
        P("ctx", None),
        P("ctx", None),
    )
    return jax.shard_map(
        body,
        mesh=mesh,
        in_specs=placed,
        out_specs=(
            P("rep", "ctx", None),
            P("rep", "ctx", None),
            P("ctx", None),
            P("ctx", None),
            P("ctx", None),
            P("ctx", None),
            P("ctx", None),
            P("ctx", None),
            P("ctx", None),
            P("ctx", None),
            P("ctx", None),
            P("ctx", None),
            P("ctx", None),
            P("ctx", None),
            P("ctx", None),
            P("ctx", None),
            P("ctx", None),
            P("ctx", None),
            P("ctx", None),
            P("ctx", None),
            P("ctx", None),
            P("ctx", None),
            P("ctx", None),
            P("ctx", None),
            P("ctx", None),
            P("ctx", None),
        ),
        check_vma=False,
    )
```

```python
import functools

import jax
import jax.numpy as jnp
import numpy as np
from jax import lax
from jax.experimental import pallas as pl
from jax.experimental.pallas import tpu as pltpu
from jax.sharding import PartitionSpec as P

MESH = pl.DeviceIdType.MESH
ANY = pl.BlockSpec(memory_space=pltpu.HBM)
VMEM = pl.BlockSpec(memory_space=pltpu.VMEM)
VMEM_BYTES = 60 * 1024 * 1024

HD = 64
STEP = 5


norm_eps = 1e-05
rope_base = 1000000.0
score_scale = 0.125
beta_one = 0.9
beta_two = 0.95
adam_eps = 1e-08


def product(left, right):
    return jnp.dot(left, right, preferred_element_type=jnp.float32)


def product_back(left, right):
    return lax.dot_general(
        left, right, (((1,), (1,)), ((), ())), preferred_element_type=jnp.float32
    )


def product_rows(left, right):
    return lax.dot_general(
        left, right, (((0,), (0,)), ((), ())), preferred_element_type=jnp.float32
    )


def rms_scale(values):
    return lax.rsqrt(jnp.mean(values * values, axis=-1, keepdims=True) + norm_eps)


def norm_back(grad, values, gain):
    scale = rms_scale(values)
    scaled = grad * gain
    inner = jnp.mean(scaled * values, axis=-1, keepdims=True)
    return (scale * scaled - values * (scale * scale * scale) * inner, grad * values * scale)


def rotary_tables(start, count, head_dim):
    half = head_dim // 2
    inverse = jnp.power(
        jnp.float32(rope_base), -(jnp.arange(half).astype(jnp.float32) * 2.0) / head_dim
    )
    angle = (start + jnp.arange(count)).astype(jnp.float32)[:, None] * inverse[None, :]
    return (jnp.cos(angle), jnp.sin(angle))


def rotary_constants(count, head_dim, seqs):
    half = head_dim // 2
    inverse = np.float32(rope_base) ** -(np.arange(half).astype(np.float32) * np.float32(2.0) / np.float32(head_dim))
    angle = np.arange(count).astype(np.float32)[:, None] * inverse.astype(np.float32)[None, :]
    cosine, sine = np.cos(angle), np.sin(angle)
    return (
        np.concatenate([cosine, cosine] * seqs, axis=1).astype(np.float32),
        np.concatenate([-sine, sine] * seqs, axis=1).astype(np.float32),
    )


def rotate(values, cosine, sine):
    half = values.shape[-1] // 2
    first = values[..., :half]
    second = values[..., half:]
    cosine = cosine[:, None, :]
    sine = sine[:, None, :]
    return jnp.concatenate(
        [first * cosine - second * sine, second * cosine + first * sine], axis=-1
    )


def rotate_back(grads, cosine, sine):
    half = grads.shape[-1] // 2
    first = grads[..., :half]
    second = grads[..., half:]
    cosine = cosine[:, None, :]
    sine = sine[:, None, :]
    return jnp.concatenate(
        [first * cosine + second * sine, second * cosine - first * sine], axis=-1
    )


def adamw(weight, grad, first, second, rate, decay):
    first_new = beta_one * first + (1.0 - beta_one) * grad
    second_new = beta_two * second + (1.0 - beta_two) * grad * grad
    fix_one = 1.0 - beta_one**STEP
    fix_two = 1.0 - beta_two**STEP
    update = first_new / fix_one / (jnp.sqrt(second_new / fix_two) + adam_eps)
    return (weight - rate * (update + decay * weight), first_new, second_new)


def swap(blocks):
    return lax.all_to_all(blocks, "ctx", 0, 0)


def gather(block):
    return lax.all_gather(block, "ctx", axis=0, tiled=False)


def scatter_sum(blocks):
    return lax.psum_scatter(blocks, "ctx", scatter_dimension=0, tiled=False)


def rep_sum(values):
    return lax.psum(values, "rep")


def rep_pairs(bit):
    return [(i, i ^ bit) for i in range(lax.axis_size("rep"))]


def rep_fold(total, bit):
    low = jnp.bfloat16
    mine = (lax.axis_index("rep") // bit) % 2
    pairs = total.reshape((total.shape[0] // 2, 2) + total.shape[1:])
    keep = lax.dynamic_index_in_dim(pairs, mine, 1, keepdims=False)
    give = lax.dynamic_index_in_dim(pairs, 1 - mine, 1, keepdims=False).astype(low)
    got = lax.ppermute(give, "rep", rep_pairs(bit))
    return keep.astype(jnp.float32) + got.astype(jnp.float32)


def rep_scatter(total, bit=1):
    while total.shape[0] > 1:
        total = rep_fold(total, bit)
        bit *= 2
    return total[0].astype(jnp.bfloat16)


def rep_gather(block):
    whole = block[None]
    bit = lax.axis_size("rep") // 2
    while bit > 0:
        mine = (lax.axis_index("rep") // bit) % 2
        got = lax.ppermute(whole, "rep", rep_pairs(bit))
        first = jnp.where(mine == 0, whole, got)
        second = jnp.where(mine == 0, got, whole)
        whole = jnp.stack([first, second], axis=1).reshape((-1,) + block.shape)
        bit //= 2
    return whole


def ring_place(index, n):
    deep = lax.div(index, 2)
    side = lax.rem(index, 2)
    return deep + side * (n - 1 - 2 * deep)


def ring_index(place, n):
    side = lax.div(place, n // 2)
    deep = place + side * (n - 1 - 2 * place)
    return 2 * deep + side


def around(place, hops, n):
    return ring_index(lax.rem(place + hops + 2 * n, n), n)


def greet(others, partners=()):
    barrier = pltpu.get_barrier_semaphore()
    for other in others:
        pl.semaphore_signal(barrier, inc=1, device_id={"ctx": other}, device_id_type=MESH)
    for other in partners:
        pl.semaphore_signal(barrier, inc=1, device_id={"rep": other}, device_id_type=MESH)
    pl.semaphore_wait(barrier, len(others) + len(partners))


def remote(source, target, send, recv, other, axis="ctx"):
    return pltpu.make_async_remote_copy(
        src_ref=source,
        dst_ref=target,
        send_sem=send,
        recv_sem=recv,
        device_id={axis: other},
        device_id_type=MESH,
    )


def rep_partners():
    place = lax.axis_index("rep")
    return place + 1 - 2 * lax.rem(place, 2), lax.rem(place + 2, 4)


class RepShare:
    def __init__(self, pieces, send, recv, own_sem):
        self.pieces, self.send, self.recv, self.own_sem = pieces, send, recv, own_sem
        self.core, self.across = rep_partners()
        self.place = lax.axis_index("rep")
        self.beyond = lax.rem(self.core + 2, 4)

    def copy(self, at, which):
        source, target = self.pieces[at]
        there = target(self.across if which == 2 else self.place)
        return remote(
            there if which == 2 else source,
            there,
            self.send.at[at, which],
            self.recv.at[at, which],
            self.across if which == 0 else self.core,
            "rep",
        )

    def own(self, at):
        source, target = self.pieces[at]
        return pltpu.make_async_copy(source, target(self.place), self.own_sem.at[at])

    def arrival(self, at, which):
        _, target = self.pieces[at]
        there = target((self.across, self.core, self.beyond)[which])
        return remote(
            there, there, self.send.at[at, which], self.recv.at[at, which], self.core, "rep"
        )

    def begin(self):
        for at in range(len(self.pieces)):
            self.copy(at, 0).start()
            self.copy(at, 1).start()
            self.own(at).start()

    def middle(self, only=None):
        for at in range(len(self.pieces)) if only is None else (only,):
            self.arrival(at, 0).wait_recv()
            self.copy(at, 2).start()

    def end(self):
        for at in range(len(self.pieces)):
            self.own(at).wait()
            for which in range(3):
                if which > 0:
                    self.arrival(at, which).wait_recv()
                self.copy(at, which).wait_send()


def add_into(total, other, step):
    @pl.loop(0, total.shape[0] // step)
    def _(at):
        here = pl.ds(pl.multiple_of(at * step, step), step)
        summed = total[here].astype(jnp.float32) + other[here].astype(jnp.float32)
        total[here] = summed.astype(total.dtype)


def add_columns(total, other, step):
    @pl.loop(0, total.shape[1] // step)
    def _(at):
        here = pl.ds(pl.multiple_of(at * step, step), step)
        summed = total[:, here].astype(jnp.float32) + other[:, here].astype(jnp.float32)
        total[:, here] = summed.astype(total.dtype)


def entry_kernel(n, head_dim, x_ref, g_ref, wq_ref, wk_ref, wv_ref, wo_ref, wg_ref, wu_ref, *refs):
    wd_ref, h_out, lin_out, g_out, o_out, q_out, wg_out, wu_out, wd_out = refs[:9]
    x_all, h_all, w_all, gain, mixed, q_own, o_own, f_own = refs[9:17]
    wq, wk, wv, wo, wf, wd, f_all, wd_low = refs[17:25]
    x_send, x_recv, p_send, p_recv, own_sem, load_sem, h_sem, r_send, r_recv, r_own = refs[25:]
    f32, low = jnp.float32, jnp.bfloat16
    me = lax.axis_index("ctx")
    place = ring_place(me, n)
    others = [lax.rem(me + hop, n) for hop in range(1, n)]
    right, left = around(place, 1, n), around(place, -1, n)
    quarter = x_ref.shape[0] // 4
    span = x_ref.shape[0] // 2
    width = x_ref.shape[1]
    share = o_own.shape[0]
    rep_rows = pl.ds(pl.multiple_of(lax.axis_index("rep") * share, 16), share)
    loads = [
        pltpu.make_async_copy(source, target, load_sem.at[at])
        for at, (source, target) in enumerate(
            (
                (wq_ref, wq),
                (wk_ref, wk),
                (wv_ref, wv),
                (wo_ref.at[rep_rows], wo),
                (wg_ref.at[rep_rows], wf.at[0]),
                (wu_ref.at[rep_rows], wf.at[1]),
                (wd_ref, wd),
            )
        )
    ]
    for at in (4, 5, 0, 1, 2, 3, 6):
        loads[at].start()
    pieces = [(x_ref, x_all, (pl.ds(part * quarter, quarter),), part < 2) for part in (0, 2, 1, 3)]
    for source, target in ((o_own, o_out), (q_own, q_out)):
        wide = source.shape[1] // 2
        pieces += [
            (source, target, (slice(None), pl.ds(part * wide, wide)), part < 1) for part in (0, 1)
        ]
    tokens, weights = range(4), range(4, len(pieces))

    def owner_of(step, up):
        return around(place, -1 - step if up else 1 + step, n)

    def hop_copy(at, step):
        source, target, where, up = pieces[at]
        owner = owner_of(step, up)
        first = isinstance(step, int) and step < 0
        return remote(
            source.at[where] if first else target.at[(owner,) + where],
            target.at[(owner,) + where],
            x_send.at[at, step + 1],
            x_recv.at[at, step + 1],
            right if up else left,
        )

    def arrived(at, step):
        _, target, where, up = pieces[at]
        block = target.at[(owner_of(step, up),) + where]
        remote(block, block, x_send.at[at, step], x_recv.at[at, step], right).wait_recv()

    def pass_first(which, step):
        for at in which:
            arrived(at, step)
            hop_copy(at, step).start()

    def pass_on(which, step):
        @pl.when(step < n - 1)
        def _():
            for at in which:
                arrived(at, step)

                @pl.when(step < n - 2)
                def _():
                    hop_copy(at, step).start()

    def swap_copy(at, hop):
        other = others[hop - 1]
        source, target = (
            (mixed.at[other], w_all.at[me]),
            (g_ref, g_out.at[me]),
            (f_own.at[other], f_all.at[:, me]),
        )[at]
        return remote(source, target, p_send.at[at, hop], p_recv.at[at, hop], other)

    own = [
        pltpu.make_async_copy(source, target, own_sem.at[at])
        for at, (source, target) in enumerate(
            (
                (x_ref, x_all.at[me]),
                (g_ref, g_out.at[me]),
                (mixed.at[me], w_all.at[me]),
                (o_own, o_out.at[me]),
                (q_own, q_out.at[me]),
                (f_own.at[me], f_all.at[:, me]),
            )
        )
    ]
    share_feed = RepShare(
        [
            (f_all.at[0], lambda r: wg_out.at[:, r]),
            (f_all.at[1], lambda r: wu_out.at[:, r]),
        ],
        r_send,
        r_recv,
        r_own,
    )
    own[0].start()
    own[1].start()
    greet(others, rep_partners())
    for at in tokens:
        hop_copy(at, -1).start()
    for copy in loads[4:6]:
        copy.wait()
    wide = f_own.shape[3]
    for owner in range(n):
        for at in (0, 1):
            f_own[owner, at] = wf[at, :, owner * wide : (owner + 1) * wide].astype(low)
    own[5].start()
    for hop in range(1, n):
        swap_copy(2, hop).start()
    pass_first(tokens, 0)
    for copy in loads[:3]:
        copy.wait()
    for source, at, wide in ((wq, 0, wq.shape[1] // n), (wk, 1, head_dim), (wv, 2, head_dim)):
        start = (0, wq.shape[1] // n, wq.shape[1] // n + head_dim)[at]
        for owner in range(n):
            mixed[owner, :, start : start + wide] = source[
                :, owner * wide : (owner + 1) * wide
            ].astype(low)
    own[2].start()
    for hop in range(1, n):
        swap_copy(0, hop).start()
        swap_copy(1, hop).start()
    columns = mixed.shape[2]
    for owner in range(n):
        q_own[:, owner * columns : (owner + 1) * columns] = mixed[owner, rep_rows]
    loads[3].wait()
    o_own[...] = wo[...].astype(low)
    own[3].start()
    own[4].start()
    for at in weights:
        hop_copy(at, -1).start()
    loads[6].wait()

    @pl.loop(0, wd.shape[0] // 16)
    def _(at):
        here = pl.ds(pl.multiple_of(at * 16, 16), 16)
        wd_low[here] = wd[here].astype(low)

    wd_give = pltpu.make_async_copy(wd_low, wd_out, own_sem.at[6])
    wd_give.start()
    pass_first(weights, 0)
    pass_first(tokens, 1)
    for hop in range(1, n):
        swap_copy(0, hop).wait_recv()
        swap_copy(1, hop).wait_recv()
    for copy in own[:3]:
        copy.wait()
    few = gain.shape[1] // n
    for owner in range(n):
        gain[:, owner * few : (owner + 1) * few] = g_out[owner, :, :few]
    heads = lin_out.shape[0]

    def give_out(step, seq):
        owner = owner_of(step, seq == 0)
        return pltpu.make_async_copy(h_all.at[owner, seq], h_out.at[owner, seq], h_sem.at[seq, step])

    def multiply(step, seq):
        owner = owner_of(step, seq == 0)
        x = x_all[owner, pl.ds(seq * span, span)].astype(f32)
        normed = (x * rms_scale(x) * gain[0:1, :width]).astype(low)
        h_all[owner, seq] = normed
        give_out(step, seq).start()
        lin = product(normed, w_all[...].reshape(width, -1))
        rows = pl.ds(pl.multiple_of(owner * span, span), span)
        for head in range(heads):
            lin_out[head, rows, seq * head_dim : (seq + 1) * head_dim] = lin[
                :, head * head_dim : (head + 1) * head_dim
            ]

    multiply(n - 1, 0)
    multiply(n - 1, 1)

    @pl.loop(0, n - 1)
    def _(step):
        @pl.when(step > 0)
        def _():
            pass_on(tokens, step + 1)

        multiply(step, 0)
        pass_on(weights, step + 1)

        @pl.when(step == 2)
        def _():
            own[5].wait()
            for hop in range(1, n):
                swap_copy(2, hop).wait_recv()
            share_feed.begin()

        @pl.when(step == n - 2)
        def _():
            share_feed.middle()

        multiply(step, 1)

    wd_give.wait()
    for copy in own[3:5]:
        copy.wait()
    for at in range(len(pieces)):
        hop_copy(at, -1).wait_send()

        @pl.loop(0, n - 2)
        def _(step):
            hop_copy(at, step).wait_send()

    @pl.loop(0, n)
    def _(step):
        give_out(step, 0).wait()
        give_out(step, 1).wait()

    for hop in range(1, n):
        swap_copy(0, hop).wait_send()
        swap_copy(1, hop).wait_send()
        swap_copy(2, hop).wait_send()
    share_feed.end()


def enter(block, gains, shards, feed_shards, w_down, head_dim):
    n = lax.axis_size("ctx")
    rows, width = block.shape
    f32, low = jnp.float32, jnp.bfloat16
    shard, q_width = shards[0].shape
    kv_width = shards[1].shape[1]
    out_width = shards[3].shape[1]
    reps = lax.axis_size("rep")
    few = shard // reps
    all_width = q_width + 2 * kv_width
    feed_width = feed_shards[0].shape[1]
    return pl.pallas_call(
        functools.partial(entry_kernel, n, head_dim),
        out_shape=[
            jax.ShapeDtypeStruct((n, 2, rows // 2, width), low),
            jax.ShapeDtypeStruct((all_width // n // head_dim, n * rows // 2, 2 * head_dim), f32),
            jax.ShapeDtypeStruct((n,) + gains.shape, f32),
            jax.ShapeDtypeStruct((n, few, out_width), low),
            jax.ShapeDtypeStruct((n, few, all_width), low),
            jax.ShapeDtypeStruct((n, reps, few, feed_width // n), low),
            jax.ShapeDtypeStruct((n, reps, few, feed_width // n), low),
            jax.ShapeDtypeStruct(w_down.shape, low),
        ],
        in_specs=[ANY] * 9,
        out_specs=[ANY, VMEM, VMEM, ANY, ANY, ANY, ANY, ANY],
        scratch_shapes=[
            pltpu.VMEM((n, rows, width), low),
            pltpu.VMEM((n, 2, rows // 2, width), low),
            pltpu.VMEM((n, shard, all_width // n), low),
            pltpu.VMEM((gains.shape[0], width + head_dim), f32),
            pltpu.VMEM((n, shard, all_width // n), low),
            pltpu.VMEM((few, all_width), low),
            pltpu.VMEM((few, out_width), low),
            pltpu.VMEM((n, 2, few, feed_width // n), low),
            pltpu.VMEM((shard, q_width), f32),
            pltpu.VMEM((shard, kv_width), f32),
            pltpu.VMEM((shard, kv_width), f32),
            pltpu.VMEM((few, out_width), f32),
            pltpu.VMEM((2, few, feed_width), f32),
            pltpu.VMEM(w_down.shape, f32),
            pltpu.VMEM((2, n, few, feed_width // n), low),
            pltpu.VMEM(w_down.shape, low),
            pltpu.SemaphoreType.DMA((8, n)),
            pltpu.SemaphoreType.DMA((8, n)),
            pltpu.SemaphoreType.DMA((3, n)),
            pltpu.SemaphoreType.DMA((3, n)),
            pltpu.SemaphoreType.DMA((7,)),
            pltpu.SemaphoreType.DMA((7,)),
            pltpu.SemaphoreType.DMA((2, n)),
            pltpu.SemaphoreType.DMA((2, 3)),
            pltpu.SemaphoreType.DMA((2, 3)),
            pltpu.SemaphoreType.DMA((2,)),
        ],
        compiler_params=pltpu.CompilerParams(
            collective_id=0, has_side_effects=True, vmem_limit_bytes=VMEM_BYTES
        ),
    )(block, gains, *shards, *feed_shards, w_down)


def lane_half(shape):
    return lax.broadcasted_iota(jnp.int32, shape, len(shape) - 1) < shape[-1] // 2


def pack(first, second):
    return jnp.where(lane_half(first.shape), first, second)


def half_mean(values):
    left = lane_half(values.shape)
    one = jnp.sum(jnp.where(left, values, 0.0), axis=-1, keepdims=True)
    two = jnp.sum(jnp.where(left, 0.0, values), axis=-1, keepdims=True)
    return jnp.where(left, one, two) * (2.0 / values.shape[-1])


def half_turn(values):
    wide = values.shape[-1]
    lane = lax.broadcasted_iota(jnp.int32, values.shape, len(values.shape) - 1)
    axis = len(values.shape) - 1
    return jnp.where(
        lax.rem(lane, wide // 2) < wide // 4,
        pltpu.roll(values, wide - wide // 4, axis),
        pltpu.roll(values, wide // 4, axis),
    )


def side_by_side(blocks, flat):
    n, count, span, wide = blocks.shape
    half = wide // 2
    left = lane_half((span, wide))

    @pl.loop(0, n // 2)
    def _(pair):
        heads = [blocks[2 * pair + at, head].astype(jnp.float32) for at in (0, 1) for head in range(count)]
        for at in range(count):
            one, two = heads[2 * at], heads[2 * at + 1]
            cols = pl.ds(pl.multiple_of((pair * count + at) * wide, wide), wide)
            flat[0:span, cols] = jnp.where(left, one, pltpu.roll(two, half, 1)).astype(flat.dtype)
            flat[span : 2 * span, cols] = jnp.where(left, pltpu.roll(one, half, 1), two).astype(
                flat.dtype
            )


def masked(scores):
    block, keys = scores.shape
    row = lax.broadcasted_iota(jnp.int32, (block, block), 0)
    seen = lax.broadcasted_iota(jnp.int32, (block, block), 1) <= row
    last = jnp.where(seen, scores[:, keys - block :], -1e30)
    return last if keys == block else jnp.concatenate([scores[:, : keys - block], last], axis=1)


def scaled(queries):
    return (queries.astype(jnp.float32) * score_scale).astype(queries.dtype)


def halves(packed):
    left = lane_half(packed.shape)
    zero = jnp.zeros_like(packed)
    return jnp.where(left, packed, zero), jnp.where(left, zero, packed)


def attend_kernel(n, group, block, lin_ref, cos_ref, sin_ref, gain_ref, x_ref, norm_ref, *refs):
    dy_ref, wo_ref = refs[:2]
    low_give, lse_give, flat_out, resid_out, next_out, dy_give, wo_out = refs[2:9]
    o_own, o_out, w_all, low_out, lse_out, dy_out = refs[9:15]
    o_send, o_recv, dy_send, dy_recv, r_send, r_recv, r_own, own_sem = refs[15:]
    f32, low = jnp.float32, jnp.bfloat16
    me = lax.axis_index("ctx")
    place = ring_place(me, n)
    others = [lax.rem(me + hop, n) for hop in range(1, n)]
    toward = (around(place, 1, n), around(place, -1, n))
    length = lin_ref.shape[1]
    span = length // n
    rows = dy_ref.shape[0] // 2
    parts = (pl.ds(0, rows), pl.ds(rows, rows))
    share = RepShare(
        [(wo_ref, lambda r: wo_out.at[:, r])],
        r_send,
        r_recv,
        r_own,
    )
    greet(others, rep_partners())

    def ring(step, side):
        owner = around(place, -step if side == 0 else step, n)
        there = dy_out.at[owner, parts[side]]
        return remote(
            there, there, dy_send.at[side, step], dy_recv.at[side, step], toward[side]
        )

    def first(side):
        return remote(
            dy_ref.at[parts[side]],
            dy_out.at[me, parts[side]],
            dy_send.at[side, 0],
            dy_recv.at[side, 0],
            toward[side],
        )

    def hop_on(step):
        for side in (0, 1):
            owner = around(place, -1 - step if side == 0 else 1 + step, n)
            there = dy_out.at[owner, parts[side]]
            remote(
                there, there, dy_send.at[side, step], dy_recv.at[side, step], toward[side]
            ).wait_recv()

            @pl.when(step < n - 2)
            def _():
                ring(step + 1, side).start()

    def give(head, hop):
        return remote(
            o_own.at[head, pl.ds(pl.multiple_of(others[hop - 1] * span, span), span)],
            o_out.at[me, head],
            o_send.at[head, hop],
            o_recv.at[head, hop],
            others[hop - 1],
        )

    for side in (0, 1):
        first(side).start()
    share.begin()
    keep_dy = pltpu.make_async_copy(dy_ref, dy_out.at[me], own_sem.at[0])
    keep_dy.start()

    for head in range(group + 1):

        @pl.loop(0, length // block)
        def _(at):
            here = pl.ds(pl.multiple_of(at * block, block), block)
            u = lin_ref[head, here]
            gain = gain_ref[0:1] if head < group else gain_ref[1:2]
            z = u * lax.rsqrt(half_mean(u * u) + norm_eps) * gain
            low_out[head, here] = (z * cos_ref[here] + half_turn(z) * sin_ref[here]).astype(low)
            if head == group:
                low_out[group + 1, here] = lin_ref[group + 1, here].astype(low)

    served = list(range(1, group * (length // block), 2))[: n - 1]

    @pl.loop(0, group)
    def _(head):
        for at in range(length // block):
            keys = (at + 1) * block
            here = pl.ds(at * block, block)
            outs, sums = [], []
            for query in halves(scaled(low_out[head, here])):
                scores = masked(product_back(query, low_out[group, :keys]))
                top = jnp.max(scores, axis=-1, keepdims=True)
                expo = jnp.exp(scores - top)
                total = jnp.sum(expo, axis=-1, keepdims=True)
                probs = (expo * (1.0 / total)).astype(low)
                outs.append(product(probs, low_out[group + 1, :keys]))
                sums.append(jnp.broadcast_to(top + jnp.log(total), (block, low_out.shape[2])))
            o_own[head, here] = pack(*outs).astype(low)
            lse_out[head, here] = pack(*sums)
            for hop, unit in enumerate(served):
                if unit % (length // block) == at:

                    @pl.when(head == unit // (length // block))
                    def _(hop=hop):
                        hop_on(hop)

            if at == 0:

                @pl.when(head == group - 1)
                def _():
                    share.middle()

        for hop in range(1, n):
            give(head, hop).start()

    gives = [
        pltpu.make_async_copy(source, target, own_sem.at[3 + at])
        for at, (source, target) in enumerate(
            ((low_out, low_give), (lse_out, lse_give), (dy_out, dy_give))
        )
    ]
    gives[0].start()
    gives[1].start()
    @pl.loop(len(served), n - 1)
    def _(step):
        hop_on(step)

    keep_dy.wait()
    gives[2].start()
    keep_o = pltpu.make_async_copy(
        o_own.at[:, pl.ds(pl.multiple_of(me * span, span), span)], o_out.at[me], own_sem.at[1]
    )
    keep_o.start()
    for side in (0, 1):
        first(side).wait_send()

        @pl.loop(1, n - 1)
        def _(step):
            ring(step, side).wait_send()

    @pl.loop(0, group)
    def _(head):
        for hop in range(1, n):
            give(head, hop).wait_send()
            source = lax.rem(me + n - hop, n)
            there = o_out.at[source, head]
            remote(
                there, there, o_send.at[head, hop], o_recv.at[head, hop], others[hop - 1]
            ).wait_recv()

    keep_o.wait()
    side_by_side(o_out, flat_out)
    share.end()
    fetch = pltpu.make_async_copy(wo_out, w_all, own_sem.at[2])
    fetch.start()
    fetch.wait()
    weights = w_all[...].reshape(-1, w_all.shape[3])
    x = x_ref[...].astype(f32)
    resid = x + product(flat_out[...], weights)
    resid_out[...] = resid
    next_out[...] = (resid * rms_scale(resid) * norm_ref[...]).astype(low)
    for copy in gives:
        copy.wait()


def attend(lin, cosine, sine, gain, tokens, norm_gain, grad, w_out):
    n = lax.axis_size("ctx")
    reps = lax.axis_size("rep")
    f32, low = jnp.float32, jnp.bfloat16
    count, length, wide = lin.shape
    group = count - 2
    return pl.pallas_call(
        functools.partial(attend_kernel, n, group, 256),
        out_shape=[
            jax.ShapeDtypeStruct((count, length, wide), low),
            jax.ShapeDtypeStruct((group, length, wide), f32),
            jax.ShapeDtypeStruct(tokens.shape, low),
            jax.ShapeDtypeStruct(tokens.shape, f32),
            jax.ShapeDtypeStruct(tokens.shape, low),
            jax.ShapeDtypeStruct((n,) + grad.shape, low),
            jax.ShapeDtypeStruct((n, reps) + w_out.shape[1:], low),
        ],
        in_specs=[VMEM] * 6 + [ANY] * 2,
        out_specs=[ANY] * 2 + [VMEM] * 3 + [ANY] * 2,
        scratch_shapes=[
            pltpu.VMEM((group, length, wide), low),
            pltpu.VMEM((n, group, length // n, wide), low),
            pltpu.VMEM((n, reps) + w_out.shape[1:], low),
            pltpu.VMEM((count, length, wide), low),
            pltpu.VMEM((group, length, wide), f32),
            pltpu.VMEM((n,) + grad.shape, low),
            pltpu.SemaphoreType.DMA((group, n)),
            pltpu.SemaphoreType.DMA((group, n)),
            pltpu.SemaphoreType.DMA((2, n)),
            pltpu.SemaphoreType.DMA((2, n)),
            pltpu.SemaphoreType.DMA((1, 3)),
            pltpu.SemaphoreType.DMA((1, 3)),
            pltpu.SemaphoreType.DMA((1,)),
            pltpu.SemaphoreType.DMA((6,)),
        ],
        compiler_params=pltpu.CompilerParams(
            collective_id=2, has_side_effects=True, vmem_limit_bytes=VMEM_BYTES
        ),
        cost_estimate=pl.CostEstimate(
            flops=16 * group * length * length * wide, bytes_accessed=2**26, transcendentals=0
        ),
    )(lin, cosine, sine, gain, tokens, norm_gain, grad, w_out)


def attend_back_kernel(n, group, block, low_src, lse_src, lin_src, cos_src, sin_src, gain_ref, b_ref, r_ref, dy_ref, *refs):
    f_ref, att_ref, wo_ref = refs[:3]
    g_keep, g_got, u_keep, u_got, d_keep, d_got, h_ref = refs[3:10]
    d_out, q_out, g_out, g_give, u_give, d_give, o_give, dr_out, f_out = refs[10:19]
    do_own, do_all, dk_sum, dv_sum, g1, g2, g3, u1, u2, u3, d1, d2, o_term, o2 = refs[19:33]
    d_own, g_swap, u_swap, h_all, q_term, q2, q_sum, g_flat, u_flat, d_sum, o_sum = refs[33:44]
    dr_low, low_ref, lse_ref, lin_ref, cos_ref, sin_ref = refs[44:50]
    do_send, do_recv, d_send, d_recv, own_sem, load_sem, x_send, x_recv = refs[50:58]
    a_send, a_recv, give_sem, head_sem = refs[58:]
    f32, low = jnp.float32, jnp.bfloat16
    me = lax.axis_index("ctx")
    others = [lax.rem(me + hop, n) for hop in range(1, n)]
    length, wide = lin_src.shape[1:]
    span = length // n

    def owned(index):
        return pl.ds(pl.multiple_of(index * span, span), span)

    def bring(head, hop):
        return remote(
            do_own.at[others[hop - 1], head],
            do_all.at[head, owned(me)],
            do_send.at[head, hop],
            do_recv.at[head, hop],
            others[hop - 1],
        )

    def give(head, hop):
        return remote(
            d_own.at[head, owned(others[hop - 1])],
            d_out.at[me, head],
            d_send.at[head, hop],
            d_recv.at[head, hop],
            others[hop - 1],
        )

    rep_place = lax.axis_index("rep")
    mine_core, mine_x = lax.rem(rep_place, 2), lax.div(rep_place, 2)
    core, across = rep_partners()
    loads = [
        pltpu.make_async_copy(source, target, load_sem.at[at])
        for at, (source, target) in enumerate(
            (
                (d_keep, d1),
                (d_got, d2),
                (g_keep, g1),
                (g_got, g2),
                (u_keep, u1),
                (u_got, u2),
                (wo_ref.at[pl.ds(0, n)], h_all.at[0]),
                (wo_ref.at[pl.ds(n, wo_ref.shape[0] - n)], h_all.at[1, pl.ds(0, wo_ref.shape[0] - n)]),
                (h_ref.at[:, 0], h_all.at[0]),
                (h_ref.at[:, 1], h_all.at[1]),
            )
        )
    ]
    head_loads = [
        pltpu.make_async_copy(source, target, head_sem.at[at])
        for at, (source, target) in enumerate(
            (
                (low_src, low_ref),
                (lse_src, lse_ref),
                (lin_src, lin_ref),
                (cos_src, cos_ref),
                (sin_src, sin_ref),
            )
        )
    ]
    for at in (6, 7, 2, 3, 4, 5, 0, 1):
        loads[at].start()
    for copy in head_loads:
        copy.start()

    def cross(at, source, target, other):
        return remote(source, target, x_send.at[at], x_recv.at[at], other, "rep")

    def crossing(at):
        if at == 5:
            return cross(5, q_term.at[:, :, 1 - mine_core], q2, core)
        if at == 4:
            return cross(4, o_term.at[:, :, 1 - mine_core], o2, core)
        if at == 0:
            return cross(0, d1.at[1 - mine_x], d_sum, across)
        source, target = ((g1, g3), (u1, u3), (o_term, o_sum))[at - 1]
        if at == 3:
            return cross(3, o_term.at[:, 1 - mine_x, mine_core], o_sum, across)
        return cross(at, source.at[:, 1 - mine_x], target, across)

    def swap_out(at, hop):
        source, target = ((g3, g_swap), (u3, u_swap))[at]
        other = others[hop - 1]
        return remote(
            source.at[other], target.at[me], a_send.at[at, hop], a_recv.at[at, hop], other
        )

    def swap_own(at):
        source, target = ((g3, g_swap), (u3, u_swap))[at]
        return pltpu.make_async_copy(source.at[me], target.at[me], own_sem.at[2 + at])

    greet(others, rep_partners())
    chunk = 64
    totals = jnp.zeros((1, f_ref.shape[1]), f32)
    for at in range(r_ref.shape[0] // chunk):
        here = pl.ds(at * chunk, chunk)
        back, terms = norm_back(b_ref[here].astype(f32), r_ref[here], f_ref[...])
        grads = dy_ref[here].astype(f32) + back
        totals += jnp.sum(terms, axis=0, keepdims=True)
        dr_out[here] = grads
        dr_low[here] = grads.astype(low)
    f_out[...] = jnp.broadcast_to(totals, f_out.shape)
    for copy in loads[6:8]:
        copy.wait()
    left = lane_half((span, wide))

    @pl.loop(0, n // 2)
    def _(pair):
        heads = []
        for at in range(group):
            index = pair * group + at
            both = product_back(dr_low[...], h_all[lax.div(index, n), lax.rem(index, n)])
            one, two = both[:span], both[span:]
            heads.append(jnp.where(left, one, pltpu.roll(two, wide // 2, 1)))
            heads.append(jnp.where(left, pltpu.roll(one, wide // 2, 1), two))
        for at, values in enumerate(heads):
            do_own[2 * pair + at // group, at % group] = values.astype(low)

    for copy in loads[8:]:
        copy.start()
    for head in range(group):
        for hop in range(1, n):
            bring(head, hop).start()
    keep_do = pltpu.make_async_copy(do_own.at[me], do_all.at[:, owned(me)], own_sem.at[0])
    keep_do.start()
    piece = d1.shape[1] // 6
    for copy in loads[2:4]:
        copy.wait()
    add_into(g1, g2, 1)
    crossing(1).start()
    for copy in loads[4:6]:
        copy.wait()
    add_into(u1, u2, 1)
    crossing(2).start()
    for copy in loads[:2]:
        copy.wait()
    add_columns(d1, d2, piece)
    crossing(0).start()
    shard = h_all.shape[3] // n

    @pl.loop(0, n // 2)
    def _(pair):
        cols = pl.ds(pl.multiple_of(pair * 2 * shard, 2 * shard), 2 * shard)
        part = product_rows(att_ref[:, cols], dr_low[...]).astype(low)
        o_term[pl.ds(2 * pair, 2)] = part.reshape(2, 2, 2, shard // 4, part.shape[1])

    crossing(4).start()
    dk_sum[...] = jnp.zeros_like(dk_sum)
    dv_sum[...] = jnp.zeros_like(dv_sum)
    g_out[...] = jnp.zeros_like(g_out)
    keep_do.wait()

    def head_back(grad, here, head, gain_at):
        turned = grad * cos_ref[here] - half_turn(grad) * sin_ref[here]
        u = lin_ref[head, here]
        scale = lax.rsqrt(half_mean(u * u) + norm_eps)
        scaled = turned * gain_ref[gain_at : gain_at + 1]
        inner = half_mean(scaled * u)
        g_out[gain_at : gain_at + 1] += jnp.sum(turned * u * scale, axis=0, keepdims=True)
        d_own[head, here] = (scale * scaled - u * (scale * scale * scale) * inner).astype(low)

    def swap_rows(at):
        first, total = ((g1, g3), (u1, u3))[at]
        crossing(1 + at).wait_recv()

        @pl.loop(0, n)
        def _(owner):
            summed = total[owner].astype(f32) + first[owner, mine_x].astype(f32)
            total[owner] = summed.astype(low)

        swap_own(at).start()
        for hop in range(1, n):
            swap_out(at, hop).start()

    swap_rows(0)
    for copy in head_loads:
        copy.wait()

    @pl.loop(0, group)
    def _(head):
        for hop in range(1, n):
            there = do_all.at[head, owned(lax.rem(me + n - hop, n))]
            remote(
                there, there, do_send.at[head, hop], do_recv.at[head, hop], others[hop - 1]
            ).wait_recv()
        for at in range(length // block):
            keys = (at + 1) * block
            here = pl.ds(at * block, block)
            query_all, grad_all = scaled(low_ref[head, here]), do_all[head, here]
            log_all = lse_ref[head, here]
            logs = (log_all[:, 0:1], log_all[:, wide // 2 : wide // 2 + 1])
            dqs, dks, dvs = [], [], []
            for query, grad, log_sum in zip(halves(query_all), halves(grad_all), logs):
                scores = masked(product_back(query, low_ref[group, :keys]))
                probs = jnp.exp(scores - log_sum)
                grad_probs = product_back(grad, low_ref[group + 1, :keys])
                both = probs * grad_probs
                inner = jnp.sum(both, axis=-1, keepdims=True)
                grad_scores = (both - probs * inner).astype(low)
                dqs.append(product(grad_scores, low_ref[group, :keys]))
                dks.append(product_rows(grad_scores, query_all))
                dvs.append(product_rows(probs.astype(low), grad_all))
            dk_sum[:keys] += pack(*dks)
            dv_sum[:keys] += pack(*dvs)
            head_back(pack(*dqs) * score_scale, here, head, 0)
        for hop in range(1, n):
            give(head, hop).start()

        @pl.when(head == 0)
        def _():
            crossing(4).wait_recv()

            @pl.loop(0, n)
            def _(owner):
                summed = o_term[owner, :, mine_core].astype(f32) + o2[owner].astype(f32)
                o_term[owner, :, mine_core] = summed.astype(low)

            crossing(3).start()
            swap_rows(1)

    @pl.loop(0, length // block)
    def _(at):
        here = pl.ds(pl.multiple_of(at * block, block), block)
        head_back(dk_sum[here], here, group, 1)
        d_own[group + 1, here] = dv_sum[here].astype(low)

    for head in (group, group + 1):
        for hop in range(1, n):
            give(head, hop).start()
    keep_d = pltpu.make_async_copy(d_own.at[:, owned(me)], d_out.at[me], own_sem.at[1])
    keep_d.start()
    for copy in loads[8:]:
        copy.wait()

    @pl.loop(0, n // 2)
    def _(pair):
        cols = pl.ds(pl.multiple_of(pair * 2 * shard, 2 * shard), 2 * shard)
        grads = jnp.concatenate([d_own[head] for head in range(group + 2)], axis=1)
        sums = [
            product_rows(h_all[seq, :, :, cols].reshape(length, 2 * shard), grads)
            for seq in (0, 1)
        ]
        both = []
        for head in range(group + 2):
            here = slice(head * wide, (head + 1) * wide)
            packed = pack(sums[0][:, here], sums[1][:, here])
            both.append(packed + pltpu.roll(packed, wide // 2, 1))
        both.append(jnp.zeros_like(both[0]))
        for at in range(0, group + 2, 2):
            part = pack(both[at], both[at + 1]).astype(low).reshape(2, 2, 2, shard // 4, wide)
            q_term[pl.ds(2 * pair, 2), :, :, :, at // 2 * wide : (at // 2 + 1) * wide] = part

    gives = [
        pltpu.make_async_copy(source, target, give_sem.at[at])
        for at, (source, target) in enumerate(
            (
                (d_sum, d_give),
                (q_sum, q_out),
                (o_sum, o_give),
                (g_flat, g_give),
                (u_flat, u_give),
            )
        )
    ]
    crossing(5).start()
    crossing(0).wait_recv()
    piece = d1.shape[1] // 6

    @pl.loop(0, 6)
    def _(at):
        here = pl.ds(pl.multiple_of(at * piece, piece), piece)
        summed = d_sum[here].astype(f32) + d1[mine_x, here].astype(f32)
        d_sum[here] = summed.astype(low)

    gives[0].start()
    crossing(5).wait_recv()

    @pl.loop(0, n)
    def _(owner):
        summed = q_term[owner, :, mine_core].astype(f32) + q2[owner].astype(f32)
        q_sum[owner] = summed.astype(low)

    gives[1].start()
    crossing(3).wait_recv()

    @pl.loop(0, n)
    def _(owner):
        summed = o_sum[owner].astype(f32) + o_term[owner, mine_x, mine_core].astype(f32)
        o_sum[owner] = summed.astype(low)

    gives[2].start()
    for at in range(6):
        crossing(at).wait_send()
    for at in (0, 1):
        swap_own(at).wait()
        for hop in range(1, n):
            swap_out(at, hop).wait()
        swapped, flat = ((g_swap, g_flat), (u_swap, u_flat))[at]
        cols = swapped.shape[2]
        for source in range(n):
            flat[:, source * cols : (source + 1) * cols] = swapped[source]
        gives[3 + at].start()

    @pl.loop(0, group)
    def _(head):
        for hop in range(1, n):
            bring(head, hop).wait_send()

    @pl.loop(0, group + 2)
    def _(head):
        for hop in range(1, n):
            give(head, hop).wait_send()
            there = d_out.at[lax.rem(me + n - hop, n), head]
            remote(
                there, there, d_send.at[head, hop], d_recv.at[head, hop], others[hop - 1]
            ).wait_recv()

    keep_d.wait()
    for copy in gives:
        copy.wait()


def attend_back(low_heads, log_sums, lin, cosine, sine, gain, above, w_output, feed_terms, normed):
    n = lax.axis_size("ctx")
    f32, low = jnp.float32, jnp.bfloat16
    count, length, wide = lin.shape
    group = count - 2
    width = normed.shape[3]
    rows_half, cols_half = feed_terms[0].shape, feed_terms[4].shape
    rows, out_width = above[4].shape
    out_half = (n, 2, rows_half[2], width)
    return pl.pallas_call(
        functools.partial(attend_back_kernel, n, group, 256),
        out_shape=[
            jax.ShapeDtypeStruct((n, count, length // n, wide), low),
            jax.ShapeDtypeStruct((n, 2, rows_half[2], (count + 1) // 2 * wide), low),
            jax.ShapeDtypeStruct(gain.shape, f32),
            jax.ShapeDtypeStruct((rows_half[2], n * rows_half[3]), low),
            jax.ShapeDtypeStruct((rows_half[2], n * rows_half[3]), low),
            jax.ShapeDtypeStruct(cols_half[1:], low),
            jax.ShapeDtypeStruct((n,) + out_half[2:], low),
            jax.ShapeDtypeStruct((rows, width), f32),
            jax.ShapeDtypeStruct((8, width), f32),
        ],
        in_specs=[ANY] * 5 + [VMEM] * 6 + [ANY] * 8,
        out_specs=[ANY, ANY, VMEM] + [ANY] * 4 + [VMEM] * 2,
        scratch_shapes=[
            pltpu.VMEM((n, group, length // n, wide), low),
            pltpu.VMEM((group, length, wide), low),
            pltpu.VMEM((length, wide), f32),
            pltpu.VMEM((length, wide), f32),
        ]
        + [pltpu.VMEM(shape, low) for shape in (rows_half, rows_half, (n,) + rows_half[2:])] * 2
        + [pltpu.VMEM(shape, low) for shape in (cols_half, cols_half)]
        + [pltpu.VMEM((n, 2) + out_half[1:], low), pltpu.VMEM(out_half, low)]
        + [
            pltpu.VMEM((count, length, wide), low),
            pltpu.VMEM((n,) + rows_half[2:], low),
            pltpu.VMEM((n,) + rows_half[2:], low),
            pltpu.VMEM((2, n, length // n, width), low),
            pltpu.VMEM((n, 2, 2, rows_half[2], (count + 1) // 2 * wide), low),
            pltpu.VMEM((n, 2, rows_half[2], (count + 1) // 2 * wide), low),
            pltpu.VMEM((n, 2, rows_half[2], (count + 1) // 2 * wide), low),
            pltpu.VMEM((rows_half[2], n * rows_half[3]), low),
            pltpu.VMEM((rows_half[2], n * rows_half[3]), low),
            pltpu.VMEM(cols_half[1:], low),
            pltpu.VMEM((n,) + out_half[2:], low),
            pltpu.VMEM((rows, width), low),
            pltpu.VMEM(low_heads.shape, low),
            pltpu.VMEM(log_sums.shape, f32),
            pltpu.VMEM(lin.shape, f32),
            pltpu.VMEM(cosine.shape, f32),
            pltpu.VMEM(sine.shape, f32),
        ]
        + [
            pltpu.SemaphoreType.DMA((group, n)),
            pltpu.SemaphoreType.DMA((group, n)),
            pltpu.SemaphoreType.DMA((count, n)),
            pltpu.SemaphoreType.DMA((count, n)),
            pltpu.SemaphoreType.DMA((4,)),
            pltpu.SemaphoreType.DMA((10,)),
            pltpu.SemaphoreType.DMA((6,)),
            pltpu.SemaphoreType.DMA((6,)),
            pltpu.SemaphoreType.DMA((2, n)),
            pltpu.SemaphoreType.DMA((2, n)),
            pltpu.SemaphoreType.DMA((5,)),
            pltpu.SemaphoreType.DMA((5,)),
        ],
        compiler_params=pltpu.CompilerParams(
            collective_id=3, has_side_effects=True, vmem_limit_bytes=VMEM_BYTES
        ),
        cost_estimate=pl.CostEstimate(
            flops=40 * group * length * length * wide, bytes_accessed=2**26, transcendentals=0
        ),
    )(low_heads, log_sums, lin, cosine, sine, gain, *above, w_output, *feed_terms, normed)


def last_kernel(n, widths, x_ref, norm_ref, f_gain, h_gain, q_sum, w_ref, b_ref, o_ref, *refs):
    g_ref, u_ref, d_ref, y_ref = refs[:4]
    dx_out, n_out, y_out, q_all, o_all, g_all, u_all, d_all = refs[4:12]
    q1, q3, q4, q5, n1, n2, n3, n4, o3, o4, blocks, flat, w_all, y_own, y_all = refs[12:27]
    load_sem, x_send, x_recv, a_send, a_recv, own_sem, y_send, y_recv = refs[27:35]
    f_send, f_recv, f_own, o_send, o_recv, o_own, q_send, q_recv, q_own = refs[35:]
    f32, low = jnp.float32, jnp.bfloat16
    me = lax.axis_index("ctx")
    others = [lax.rem(me + hop, n) for hop in range(1, n)]
    mine_x = lax.div(lax.axis_index("rep"), 2)
    core, across = rep_partners()
    loads = (
        pltpu.make_async_copy(q_sum.at[:, mine_x], q1, load_sem.at[0]),
        pltpu.make_async_copy(b_ref, blocks, load_sem.at[1]),
        pltpu.make_async_copy(w_ref, w_all, load_sem.at[2]),
    )
    y_load = pltpu.make_async_copy(y_ref, y_own, load_sem.at[3])
    y_load.start()
    for copy in loads:
        copy.start()
    place = ring_place(me, n)
    toward = (around(place, 1, n), around(place, -1, n))
    y_half = y_own.shape[1] // 2
    y_parts = (pl.ds(0, y_half), pl.ds(y_half, y_half))

    def y_copy(step, side):
        source = y_own if step == 0 else y_all
        return remote(
            source.at[step, y_parts[side]],
            y_all.at[step + 1, y_parts[side]],
            y_send.at[side, step + 1],
            y_recv.at[side, step + 1],
            toward[side],
        )

    def y_hop(step):
        if step > 0:
            for side in (0, 1):
                y_copy(step - 1, side).wait_recv()
            summed = y_all[step].astype(f32) + y_own[step].astype(f32)
            (y_out if step == n - 1 else y_all.at[step])[...] = summed.astype(low)
        if step < n - 1:
            for side in (0, 1):
                y_copy(step, side).start()

    def cross(at, source, target, other):
        return remote(source, target, x_send.at[at], x_recv.at[at], other, "rep")

    steps = (
        cross(0, q_sum.at[:, 1 - mine_x], q3, across),
        cross(1, n1, n2, core),
        cross(2, n2, n3, across),
    )

    def swap_out(at, hop):
        source, target = ((o_ref, o3), (q3, q4), (n3, n4))[at]
        other = others[hop - 1]
        return remote(
            source if at == 2 else source.at[other],
            target.at[me],
            a_send.at[at, hop],
            a_recv.at[at, hop],
            other,
        )

    def swap_own(at):
        source, target = ((o_ref, o3), (q3, q4), (n3, n4))[at]
        return pltpu.make_async_copy(
            source if at == 2 else source.at[me], target.at[me], own_sem.at[at]
        )

    def swap_all(at):
        swap_own(at).start()
        for hop in range(1, n):
            swap_out(at, hop).start()

    def swapped(at):
        swap_own(at).wait()
        for hop in range(1, n):
            swap_out(at, hop).wait()

    few = o4.shape[0]
    quarter = d_ref.shape[1]

    def rows_of(target):
        return lambda r: target.at[pl.ds(pl.multiple_of(r * few, 16), few)]

    feed = RepShare(
        [
            (g_ref, rows_of(g_all)),
            (u_ref, rows_of(u_all)),
            (d_ref, lambda r: d_all.at[:, pl.ds(pl.multiple_of(r * quarter, quarter), quarter)]),
        ],
        f_send,
        f_recv,
        f_own,
    )
    last_q = RepShare([(q5, rows_of(q_all))], q_send, q_recv, q_own)
    last_o = RepShare([(o4, rows_of(o_all))], o_send, o_recv, o_own)

    greet(others, rep_partners())
    steps[0].start()
    feed.begin()
    y_load.wait()
    y_hop(0)
    swap_all(0)
    for copy in loads:
        copy.wait()
    side_by_side(blocks, flat)
    rows, width = x_ref.shape
    tile = 256

    @pl.loop(0, width // tile)
    def _(at):
        cols = pl.ds(pl.multiple_of(at * tile, tile), tile)
        dx_out[:, cols] = product_back(flat[...], w_rows(w_all, at, tile))

    y_hop(1)
    steps[0].wait()

    @pl.loop(0, n)
    def _(owner):
        q3[owner] = (q3[owner].astype(f32) + q1[owner].astype(f32)).astype(low)

    swap_all(1)
    y_hop(2)
    n1[...] = jnp.zeros_like(n1)
    chunk = 64
    totals = jnp.zeros((1, width), f32)
    for at in range(rows // chunk):
        here = pl.ds(at * chunk, chunk)
        x = x_ref[here].astype(f32)
        back, terms = norm_back(dx_out[here], x, norm_ref[...])
        totals += jnp.sum(terms, axis=0, keepdims=True)
        dx_out[here] = back
    lanes = n1.shape[1]
    lines = width // lanes
    for at in range(lines):
        here = slice(at * lanes, (at + 1) * lanes)
        n1[at : at + 1] = totals[:, here]
        n1[lines + at : lines + at + 1] = f_gain[:, here]
    heads = h_gain[0:2]
    heads = heads + pltpu.roll(heads, lanes // 2, 1)
    n1[2 * lines : 2 * lines + 1] = pack(heads[0:1], heads[1:2])
    steps[1].start()
    y_hop(3)
    steps[1].wait()
    n2[...] += n1[...]
    steps[2].start()
    feed.middle(0)
    y_hop(4)
    swapped(1)
    q_wide, k_wide = widths
    for source in range(n):
        at = 0
        place = 0
        for wide in (q_wide, k_wide, k_wide):
            start = place + source * wide
            q5[:, start : start + wide] = q4[source, :, at : at + wide]
            at += wide
            place += n * wide
    last_q.begin()
    y_hop(5)
    feed.middle(1)
    swapped(0)

    @pl.loop(0, few // 16)
    def _(at):
        here = pl.ds(pl.multiple_of(at * 16, 16), 16)
        total = o3[0, here].astype(f32)
        for source in range(1, n):
            total += o3[source, here].astype(f32)
        o4[here] = total.astype(low)

    last_o.begin()
    y_hop(6)
    steps[2].wait()
    n3[...] += n2[...]
    swap_all(2)
    feed.middle(2)
    last_q.middle()
    last_o.middle()
    for step in range(7, n):
        y_hop(step)
    swapped(2)
    total = n4[0]
    for source in range(1, n):
        total += n4[source]
    n_out[...] = total
    feed.end()
    last_q.end()
    last_o.end()
    for step in range(n - 1):
        for side in (0, 1):
            y_copy(step, side).wait_send()


def w_rows(w_all, at, tile):
    n, reps, few, cols = w_all.shape
    rows = [w_all[lax.div(at * tile + start, reps * few), lax.rem(lax.div(at * tile + start, few), reps),
                  pl.ds(pl.multiple_of(lax.rem(at * tile + start, few), 16), 16)]
            for start in range(0, tile, 16)]
    return jnp.concatenate(rows, axis=0)


def last_sums(x, norm_gain, ffn_terms, head_terms, q_sum, w_full, blocks, parts, widths):
    o_part, g_part, u_part, d_part, y_part = parts
    n = lax.axis_size("ctx")
    reps = lax.axis_size("rep")
    f32, low = jnp.float32, jnp.bfloat16
    few, wide = q_sum.shape[2:]
    rows, width = x.shape
    shard = reps * few
    out_wide = o_part.shape[2]
    feed_wide = g_part.shape[1]
    lines = -(-(2 * width // 128 + 1) // 8) * 8
    return pl.pallas_call(
        functools.partial(last_kernel, n, widths),
        out_shape=[
            jax.ShapeDtypeStruct((rows, width), f32),
            jax.ShapeDtypeStruct((lines, 128), f32),
            jax.ShapeDtypeStruct(y_part.shape[1:], low),
            jax.ShapeDtypeStruct((shard, w_full.shape[3]), low),
            jax.ShapeDtypeStruct((shard, out_wide), low),
            jax.ShapeDtypeStruct((shard, feed_wide), low),
            jax.ShapeDtypeStruct((shard, feed_wide), low),
            jax.ShapeDtypeStruct((d_part.shape[0], reps * d_part.shape[1]), low),
        ],
        in_specs=[VMEM] * 4 + [ANY] * 8,
        out_specs=[VMEM] * 3 + [ANY] * 5,
        scratch_shapes=[
            pltpu.VMEM((n, few, wide), low),
            pltpu.VMEM((n, few, wide), low),
            pltpu.VMEM((n, few, wide), low),
            pltpu.VMEM((few, w_full.shape[3]), low),
            pltpu.VMEM((lines, 128), f32),
            pltpu.VMEM((lines, 128), f32),
            pltpu.VMEM((lines, 128), f32),
            pltpu.VMEM((n, lines, 128), f32),
            pltpu.VMEM((n, few, out_wide), low),
            pltpu.VMEM((few, out_wide), low),
            pltpu.VMEM(blocks.shape, low),
            pltpu.VMEM((rows, w_full.shape[3]), low),
            pltpu.VMEM(w_full.shape, low),
            pltpu.VMEM(y_part.shape, low),
            pltpu.VMEM(y_part.shape, low),
            pltpu.SemaphoreType.DMA((4,)),
            pltpu.SemaphoreType.DMA((3,)),
            pltpu.SemaphoreType.DMA((3,)),
            pltpu.SemaphoreType.DMA((3, n)),
            pltpu.SemaphoreType.DMA((3, n)),
            pltpu.SemaphoreType.DMA((3,)),
            pltpu.SemaphoreType.DMA((2, n)),
            pltpu.SemaphoreType.DMA((2, n)),
        ]
        + [
            pltpu.SemaphoreType.DMA(shape)
            for k in (3, 1, 1)
            for shape in ((k, 3), (k, 3), (k,))
        ],
        compiler_params=pltpu.CompilerParams(
            collective_id=4, has_side_effects=True, vmem_limit_bytes=VMEM_BYTES
        ),
    )(x, norm_gain, ffn_terms, head_terms, q_sum, w_full, blocks, *parts)


def feed_kernel(n, tile, normed_ref, grad_ref, wg_src, wu_src, wd_src, wq_ref, *refs):
    y_out, y_hold, b_out, wq_out, g_keep, g_got, u_keep, u_got, d_keep, d_got = refs[:10]
    h_slots, d_slots, y_slots, b_slots, hid, dgate, dup, dwg, dwu, dwd, stage, d_stage, y_stage = refs[10:23]
    wg_ref, wu_ref, wd_ref = refs[23:26]
    h_send, h_recv, y_send, y_recv, b_send, b_recv, d_sem, own_sem, r_send, r_recv, r_own = refs[26:37]
    keep_sem, c_send, c_recv, dc_send, dc_recv, y_sem = refs[37:]
    f32, low = jnp.float32, jnp.bfloat16
    me = lax.axis_index("ctx")
    place = ring_place(me, n)
    right, left = around(place, 1, n), around(place, -1, n)
    rows, width = normed_ref.shape
    half = rows // 2
    parts = (pl.ds(0, half), pl.ds(half, half))
    toward = (right, left)

    def grad_load(step, side):
        owner = around(place, -1 - step if side == 0 else 1 + step, n)
        return pltpu.make_async_copy(
            grad_ref.at[owner, parts[side]],
            d_slots.at[lax.rem(step, 2), parts[side]],
            d_sem.at[lax.rem(step, 2), side],
        )

    def pass_on(step, side):
        return remote(
            h_slots.at[step, parts[side]],
            h_slots.at[step + 1, parts[side]],
            h_send.at[side, step + 1],
            h_recv.at[side, step + 1],
            toward[side],
        )

    def sum_on(slots, send, recv, step, side):
        return remote(
            slots.at[step, parts[side]],
            slots.at[step + 1, parts[side]],
            send.at[side, step + 1],
            recv.at[side, step + 1],
            toward[side],
        )

    def first(side):
        return remote(
            normed_ref.at[parts[side]],
            h_slots.at[0, parts[side]],
            h_send.at[side, 0],
            h_recv.at[side, 0],
            toward[side],
        )

    weight_loads = [
        pltpu.make_async_copy(source, target, own_sem.at[5 + at])
        for at, (source, target) in enumerate(
            ((wg_src, wg_ref), (wu_src, wu_ref), (wd_src, wd_ref))
        )
    ]
    for copy in weight_loads:
        copy.start()
    for side in (0, 1):
        grad_load(0, side).start()
    keep = pltpu.make_async_copy(normed_ref, h_slots.at[n - 1], own_sem.at[0])
    keep.start()
    share = RepShare([(wq_ref, lambda r: wq_out.at[:, r])], r_send, r_recv, r_own)
    greet((left, right), rep_partners())
    for side in (0, 1):
        first(side).start()
    share.begin()
    y_slots[0] = jnp.zeros(y_slots.shape[1:], low)
    b_slots[0] = jnp.zeros((rows, width), low)

    @pl.loop(0, width // tile)
    def _(at):
        cols = pl.ds(pl.multiple_of(at * tile, tile), tile)
        dwg[cols, :] = jnp.zeros((tile, dwg.shape[1]), f32)
        dwu[cols, :] = jnp.zeros((tile, dwu.shape[1]), f32)
        dwd[:, cols] = jnp.zeros((dwd.shape[0], tile), f32)

    keep.wait()
    for copy in weight_loads:
        copy.wait()

    def next_block(step):
        for side in (0, 1):
            block = h_slots.at[step, parts[side]]
            remote(block, block, h_send.at[side, step], h_recv.at[side, step], right).wait_recv()

            @pl.when(step < n - 2)
            def _():
                pass_on(step, side).start()

    def hold(step):
        turn = lax.rem(step, 2)
        return pltpu.make_async_copy(y_stage.at[turn], y_hold.at[step], y_sem.at[turn])

    next_block(0)
    kept = y_slots.shape[2] // tile

    @pl.loop(0, n)
    def _(step):
        @pl.when(step < n - 1)
        def _():
            for side in (0, 1):
                grad_load(step + 1, side).start()

        for side in (0, 1):
            grad_load(step, side).wait()

        @pl.when(step == n // 2)
        def _():
            share.middle()

        turn = lax.rem(step, 2)
        h = h_slots[step]
        gate = jnp.dot(h, wg_ref[...], preferred_element_type=f32)
        up = jnp.dot(h, wu_ref[...], preferred_element_type=f32)
        grad_hidden = product_back(d_slots[turn], wd_ref[...])
        sigma = jax.nn.sigmoid(gate)
        silu = gate * sigma
        hid[...] = (silu * up).astype(low)
        dup[...] = (grad_hidden * silu).astype(low)
        dgate[...] = (grad_hidden * up * sigma * (1.0 + gate * (1.0 - sigma))).astype(low)

        @pl.when(step < n - 2)
        def _():
            next_block(step + 1)

        @pl.when(step > 0)
        def _():
            for side in (0, 1):
                sum_on(b_slots, b_send, b_recv, step - 1, side).wait_recv()

        @pl.loop(0, width // tile)
        def _(at):
            cols = pl.ds(pl.multiple_of(at * tile, tile), tile)
            back = product_back(dgate[...], wg_ref[cols, :]) + product_back(
                dup[...], wu_ref[cols, :]
            )
            b_slots[step, :, cols] = (b_slots[step, :, cols].astype(f32) + back).astype(low)

        @pl.when(step < n - 1)
        def _():
            for side in (0, 1):
                sum_on(b_slots, b_send, b_recv, step, side).start()

        @pl.when(step > 0)
        def _():
            for side in (0, 1):
                sum_on(y_slots, y_send, y_recv, step - 1, side).wait_recv()

        @pl.loop(0, kept)
        def _(at):
            cols = pl.ds(pl.multiple_of(at * tile, tile), tile)
            added = jnp.dot(hid[...], wd_ref[:, cols], preferred_element_type=f32)
            y_slots[step, :, cols] = (y_slots[step, :, cols].astype(f32) + added).astype(low)

        @pl.when(step < n - 1)
        def _():
            for side in (0, 1):
                sum_on(y_slots, y_send, y_recv, step, side).start()

        @pl.when(step >= 2)
        def _():
            hold(step - 2).wait()

        @pl.loop(kept, width // tile)
        def _(at):
            cols = pl.ds(pl.multiple_of(at * tile, tile), tile)
            there = pl.ds(pl.multiple_of((at - kept) * tile, tile), tile)
            added = jnp.dot(hid[...], wd_ref[:, cols], preferred_element_type=f32)
            y_stage[turn, :, there] = added.astype(low)

        hold(step).start()

        @pl.loop(0, width // tile)
        def _(at):
            cols = pl.ds(pl.multiple_of(at * tile, tile), tile)
            h_cols = h_slots[step, :, cols]
            dwg[cols, :] += product_rows(h_cols, dgate[...])
            dwu[cols, :] += product_rows(h_cols, dup[...])
            dwd[:, cols] += product_rows(hid[...], d_slots[turn, :, cols])

    outs = (
        pltpu.make_async_copy(y_slots.at[n - 1], y_out, own_sem.at[1]),
        pltpu.make_async_copy(b_slots.at[n - 1], b_out, own_sem.at[2]),
    )
    for copy in outs:
        copy.start()
    hold(n - 2).wait()
    hold(n - 1).wait()
    core, _ = rep_partners()
    mine = lax.rem(lax.axis_index("rep"), 2)
    wide = width // 4
    few = g_keep.shape[2]

    def column_copies(side):
        quarter = (2 * side + mine, 2 * side + 1 - mine)
        return quarter, (
            pltpu.make_async_copy(d_stage.at[2 * side], d_keep.at[side], own_sem.at[3 + side]),
            remote(
                d_stage.at[2 * side + 1],
                d_got.at[side],
                dc_send.at[side],
                dc_recv.at[side],
                core,
                "rep",
            ),
        )

    for side in (0, 1):
        quarters, copies = column_copies(side)
        for at, (quarter, copy) in enumerate(zip(quarters, copies)):
            cols = pl.ds(pl.multiple_of(quarter * wide, wide), wide)
            d_stage[2 * side + at] = dwd[:, cols].astype(low)
            copy.start()

    def row_copies(owner, turn):
        for at, (total, keep, got) in enumerate(((dwg, g_keep, g_got), (dwu, u_keep, u_got))):
            for side in (0, 1):
                slot = 4 * at + 2 * side
                yield total, slot, 2 * side + mine, pltpu.make_async_copy(
                    stage.at[turn, slot], keep.at[owner, side], keep_sem.at[turn, slot // 2]
                )
                yield total, slot + 1, 2 * side + 1 - mine, remote(
                    stage.at[turn, slot + 1],
                    got.at[owner, side],
                    c_send.at[owner, slot // 2],
                    c_recv.at[owner, slot // 2],
                    core,
                    "rep",
                )

    def row_wait(owner, turn):
        for _, slot, _, copy in row_copies(owner, turn):
            if slot % 2 == 0:
                copy.wait()
            else:
                copy.wait_send()

    @pl.loop(0, n)
    def _(owner):
        turn = lax.rem(owner, 2)

        @pl.when(owner >= 2)
        def _():
            row_wait(owner - 2, turn)

        for total, slot, quarter, copy in row_copies(owner, turn):
            start = pl.multiple_of((4 * owner + quarter) * few, 8)
            stage[turn, slot] = total[pl.ds(start, few), :].astype(low)
            copy.start()

    for owner in (n - 2, n - 1):
        row_wait(owner, owner % 2)

    @pl.loop(0, n)
    def _(owner):
        for _, slot, _, copy in row_copies(owner, 0):
            if slot % 2 == 1:
                copy.wait_recv()

    for side in (0, 1):
        for copy in column_copies(side)[1]:
            copy.wait()
    for copy in outs:
        copy.wait()
    share.end()
    for side in (0, 1):
        first(side).wait_send()

        @pl.loop(0, n - 2)
        def _(step):
            pass_on(step, side).wait_send()

        @pl.loop(0, n - 1)
        def _(step):
            sum_on(b_slots, b_send, b_recv, step, side).wait_send()
            sum_on(y_slots, y_send, y_recv, step, side).wait_send()


def feed_scratch(n, rows, width, cols):
    low = jnp.bfloat16
    return [
        pltpu.VMEM((n, rows, width), low),
        pltpu.VMEM((2, rows, width), low),
        pltpu.VMEM((n, rows, width // 2), low),
        pltpu.VMEM((n, rows, width), low),
        pltpu.VMEM((rows, cols), low),
        pltpu.VMEM((rows, cols), low),
        pltpu.VMEM((rows, cols), low),
        pltpu.VMEM((width, cols), jnp.float32),
        pltpu.VMEM((width, cols), jnp.float32),
        pltpu.VMEM((cols, width), jnp.float32),
        pltpu.VMEM((2, 8, width // (4 * n), cols), low),
        pltpu.VMEM((4, cols, width // 4), low),
        pltpu.VMEM((2, rows, width // 2), low),
        pltpu.VMEM((width, cols), low),
        pltpu.VMEM((width, cols), low),
        pltpu.VMEM((cols, width), low),
    ]


def feed_fits(n, rows, width, cols):
    wide = -(-cols // 128) * 128
    slots = (3 * n + 2) * rows * width * 2 + 3 * rows * wide * 2
    weights = 3 * width * wide * (2 + 4) + 4 * width * wide * 2 // n + width * wide * 2
    return slots + weights + 24 * rows * wide <= VMEM_BYTES


def feed_ring(normed, grad_all, w_gate, w_up, w_down, quarter):
    n = lax.axis_size("ctx")
    rows, width = normed.shape
    cols = w_gate.shape[1]
    low = jnp.bfloat16
    reps = lax.axis_size("rep")
    return pl.pallas_call(
        functools.partial(feed_kernel, n, 256),
        out_shape=[
            jax.ShapeDtypeStruct((rows, width // 2), low),
            jax.ShapeDtypeStruct((n, rows, width // 2), low),
            jax.ShapeDtypeStruct((rows, width), low),
            jax.ShapeDtypeStruct((n, reps) + quarter.shape[1:], quarter.dtype),
        ]
        + [jax.ShapeDtypeStruct((n, 2, width // (4 * n), cols), low)] * 4
        + [jax.ShapeDtypeStruct((2, cols, width // 4), low)] * 2,
        in_specs=[ANY] * 6,
        out_specs=[ANY] * 10,
        scratch_shapes=feed_scratch(n, rows, width, cols)
        + [pltpu.SemaphoreType.DMA((2, n))] * 6
        + [pltpu.SemaphoreType.DMA((2, 2)), pltpu.SemaphoreType.DMA((8,))]
        + [pltpu.SemaphoreType.DMA((1, 3))] * 2
        + [pltpu.SemaphoreType.DMA((1,))]
        + [pltpu.SemaphoreType.DMA((2, 4))]
        + [pltpu.SemaphoreType.DMA((n, 4))] * 2
        + [pltpu.SemaphoreType.DMA((2,))] * 3,
        compiler_params=pltpu.CompilerParams(
            collective_id=1, has_side_effects=True, vmem_limit_bytes=VMEM_BYTES
        ),
        cost_estimate=pl.CostEstimate(
            flops=18 * n * rows * width * cols, bytes_accessed=40 * width * cols, transcendentals=0
        ),
    )(normed, grad_all, w_gate, w_up, w_down, quarter)


def columns_by_owner(shard, parts):
    rows, width = shard.shape
    return shard.reshape(rows, parts, width // parts).transpose(1, 0, 2)


def columns_joined(blocks):
    parts, rows, width = blocks.shape
    return blocks.transpose(1, 0, 2).reshape(rows, parts * width)


def take_gains(gains, width):
    gains = gains.astype(jnp.float32)
    return gains[:width, 0], gains[:width, 1], gains[width:, 0], gains[width:, 1]


class HeadAttention:
    def __init__(self, dims, shards, feed_shards, w_down, gains_shard, tokens, cotangent):
        self.dims = dims
        parts, seqs, span, width, head_dim, heads, kv_heads = dims
        low = jnp.bfloat16
        group = heads // kv_heads
        self.group = group
        rows = seqs * span
        length = parts * span
        few = gains_shard.shape[0]
        padded = jnp.pad(gains_shard.astype(low).astype(jnp.float32).T, ((0, 6), (0, -few % 128)))
        (
            self.normed,
            self.lin,
            gains_all,
            out_quarter,
            self.quarter,
            w_gate,
            w_up,
            self.w_down,
        ) = enter(tokens.reshape(rows, width), padded, shards, feed_shards, w_down, head_dim)
        gains = gains_all[:, :2, :few].transpose(0, 2, 1).reshape(-1, 2)
        self.gain_attn, self.gain_ffn, gain_query, gain_key = take_gains(gains, width)
        self.cosine, self.sine = (
            jnp.asarray(table) for table in rotary_constants(length, head_dim, seqs)
        )
        self.gain = jnp.pad(
            jnp.stack([jnp.concatenate([g] * seqs) for g in (gain_query, gain_key)]), ((0, 6), (0, 0))
        )
        self.tokens = tokens.reshape(rows, width)
        (
            self.low_heads,
            self.log_sums,
            self.attended,
            self.resid,
            self.normed_two,
            self.grad_all,
            w_output,
        ) = attend(
            self.lin,
            self.cosine,
            self.sine,
            self.gain,
            self.tokens,
            self.gain_ffn[None],
            cotangent.reshape(rows, width),
            out_quarter,
        )
        self.w_output = w_output.reshape(width, -1)
        self.w_gate = w_gate.reshape(width, -1)
        self.w_up = w_up.reshape(width, -1)

    def feed(self):
        self.added, self.held, back, self.w_full, *self.feed_terms = feed_ring(
            self.normed_two, self.grad_all, self.w_gate, self.w_up, self.w_down, self.quarter
        )
        return back

    def backward(self, normed_two_grad, grad_low):
        span, width = self.dims[2:4]
        self.blocks, self.q_sum, self.head_terms, *parts_done, grad_resid, ffn_terms = attend_back(
            self.low_heads,
            self.log_sums,
            self.lin,
            self.cosine,
            self.sine,
            self.gain,
            (normed_two_grad, self.resid, grad_low, self.gain_ffn[None], self.attended),
            self.w_output.reshape(-1, span, width),
            self.feed_terms,
            self.normed,
        )
        self.parts_done = parts_done
        return grad_resid, ffn_terms[0]

    def finish(self, grad_resid, ffn_terms):
        parts, seqs, span, width, head_dim, heads, kv_heads = self.dims
        gate, up, down, out = self.parts_done
        back, gains, added, mixed, out, gate, up, down = last_sums(
            self.tokens,
            self.gain_attn[None],
            ffn_terms[None],
            self.head_terms,
            self.q_sum,
            self.w_full,
            self.blocks,
            (out, gate, up, down, self.held),
            (self.group * head_dim, head_dim),
        )
        gains = gains.reshape(-1)
        one, two = gains[:width], gains[width : 2 * width]
        query = gains[2 * width : 2 * width + head_dim]
        key = gains[2 * width + head_dim : 2 * width + 2 * head_dim]
        gains = jnp.stack([jnp.concatenate([one, query]), jnp.concatenate([two, key])], axis=1)
        count = gains.shape[0] // parts
        gains = lax.dynamic_slice_in_dim(gains, lax.axis_index("ctx") * count, count, 0)
        cuts = (heads * head_dim, (heads + kv_heads) * head_dim)
        grads = (
            mixed[:, : cuts[0]], mixed[:, cuts[0] : cuts[1]], mixed[:, cuts[1] :], out, gate, up, down, gains
        )
        added = jnp.concatenate([self.added, added], axis=1).astype(jnp.float32)
        return grad_resid + back, self.resid + added, grads


class RowAttention:
    def __init__(self, dims, shards, feed_shards, w_down, gains_shard, tokens, cotangent):
        self.dims = dims
        parts, seqs, span, width, head_dim, heads, kv_heads = dims
        low = jnp.bfloat16
        gains = lax.all_gather(gains_shard.astype(low), "ctx", axis=0, tiled=True)
        self.gain_attn, self.gain_ffn, self.gain_query, self.gain_key = take_gains(gains, width)
        place = lax.axis_index("ctx")
        rows = seqs * span
        self.group = heads // kv_heads
        self.weights = tuple(
            lax.all_gather(w.astype(low), "ctx", axis=0, tiled=True) for w in shards[:3]
        )
        self.w_output = lax.all_gather(shards[3].astype(low), "ctx", axis=0, tiled=True)
        self.w_gate, self.w_up = (
            swap(columns_by_owner(w.astype(low), parts)).reshape(width, -1) for w in feed_shards
        )
        self.w_down = w_down.astype(low)
        self.grad_all = gather(cotangent.reshape(rows, width))
        inputs = tokens.astype(jnp.float32).reshape(rows, width)
        self.normed = (inputs * rms_scale(inputs) * self.gain_attn).astype(jnp.bfloat16)
        query_lin, key_lin, value_lin = (product(self.normed, w) for w in self.weights)
        self.cosine, self.sine = rotary_tables(place * span, span, head_dim)
        self.query_heads = query_lin.reshape(seqs, span, heads, head_dim)
        query_low = rotate(
            self.query_heads * rms_scale(self.query_heads) * self.gain_query, self.cosine, self.sine
        ).astype(jnp.bfloat16)
        self.key_heads = key_lin.reshape(seqs, span, kv_heads, head_dim)
        key_low = rotate(
            self.key_heads * rms_scale(self.key_heads) * self.gain_key, self.cosine, self.sine
        ).astype(jnp.bfloat16)
        kv_width = kv_heads * head_dim
        self.keys_all = lax.all_gather(
            key_low.reshape(seqs, span, kv_width), "ctx", axis=1, tiled=True
        )
        self.values_all = lax.all_gather(
            value_lin.astype(jnp.bfloat16).reshape(seqs, span, kv_width), "ctx", axis=1, tiled=True
        )
        self.query_grouped = query_low.reshape(seqs, span, kv_heads, self.group, head_dim)
        query_pos = place * span + jnp.arange(span)
        self.visible = jnp.arange(parts * span)[None, :] <= query_pos[:, None]
        self.attended = self.forward()
        self.resid = inputs + product(self.attended, self.w_output)
        normed_two = self.resid * rms_scale(self.resid) * self.gain_ffn
        self.normed_two = normed_two.astype(jnp.bfloat16)
        self.tokens = inputs

    def feed(self):
        self.added, back, *self.feed_terms = feed_plain(
            self.normed_two, self.grad_all, self.w_gate, self.w_up, self.w_down
        )
        return back

    def head_scores(self, index):
        head_dim = self.dims[4]
        query_group = lax.dynamic_index_in_dim(self.query_grouped, index, 2, keepdims=False)
        key_group = lax.dynamic_slice_in_dim(self.keys_all, index * head_dim, head_dim, 2)
        value_group = lax.dynamic_slice_in_dim(self.values_all, index * head_dim, head_dim, 2)
        raw = (
            jnp.einsum("scjd,skd->sjck", query_group, key_group, preferred_element_type=jnp.float32)
            * score_scale
        )
        return (query_group, key_group, value_group, jnp.where(self.visible, raw, -1e30))

    def forward(self):
        parts, seqs, span, width, head_dim, heads, kv_heads = self.dims

        def forward_head(index, carry):
            attended, log_sums = carry
            _, _, value_group, scores = self.head_scores(index)
            top = jnp.max(scores, axis=-1, keepdims=True)
            expo = jnp.exp(scores - top)
            total = jnp.sum(expo, axis=-1, keepdims=True)
            probs = (expo / total).astype(jnp.bfloat16)
            head_out = jnp.einsum(
                "sjck,skd->scjd", probs, value_group, preferred_element_type=jnp.float32
            )
            attended = lax.dynamic_update_index_in_dim(attended, head_out, index, 2)
            log_sums = lax.dynamic_update_index_in_dim(
                log_sums, (top + jnp.log(total))[..., 0], index, 0
            )
            return (attended, log_sums)

        attended, self.log_sums = lax.fori_loop(
            0,
            kv_heads,
            forward_head,
            (
                jnp.zeros((seqs, span, kv_heads, self.group, head_dim), jnp.float32),
                jnp.zeros((kv_heads, seqs, self.group, span), jnp.float32),
            ),
        )
        return attended.reshape(seqs * span, heads * head_dim).astype(jnp.bfloat16)

    def backward(self, normed_two_grad, grad_low):
        back_two, ffn_terms = norm_back(
            normed_two_grad.astype(jnp.float32), self.resid, self.gain_ffn
        )
        grad_resid = grad_low.astype(jnp.float32) + back_two
        resid_low = grad_resid.astype(jnp.bfloat16)
        self.out_term = product_rows(self.attended, resid_low)
        self.heads_backward(product_back(resid_low, self.w_output).astype(jnp.bfloat16))
        return grad_resid, jnp.sum(ffn_terms, axis=0)

    def heads_backward(self, grad_rows):
        parts, seqs, span, width, head_dim, heads, kv_heads = self.dims
        group = self.group
        rows = seqs * span
        length = parts * span
        kv_width = kv_heads * head_dim
        grad_grouped = grad_rows.reshape(seqs, span, kv_heads, group, head_dim)

        def backward_head(index, carry):
            query_acc, key_acc, value_acc = carry
            query_group, key_group, value_group, scores = self.head_scores(index)
            log_group = lax.dynamic_index_in_dim(self.log_sums, index, 0, keepdims=False)
            probs = jnp.exp(scores - log_group[..., None])
            grad_group = lax.dynamic_index_in_dim(grad_grouped, index, 2, keepdims=False)
            grad_probs = jnp.einsum(
                "scjd,skd->sjck", grad_group, value_group, preferred_element_type=jnp.float32
            )
            inner = jnp.sum(probs * grad_probs, axis=-1, keepdims=True)
            grad_scores = (probs * (grad_probs - inner)).astype(jnp.bfloat16)
            grad_query = (
                jnp.einsum(
                    "sjck,skd->scjd", grad_scores, key_group, preferred_element_type=jnp.float32
                )
                * score_scale
            )
            grad_key = (
                jnp.einsum(
                    "sjck,scjd->skd", grad_scores, query_group, preferred_element_type=jnp.float32
                )
                * score_scale
            )
            grad_value = jnp.einsum(
                "sjck,scjd->skd",
                probs.astype(jnp.bfloat16),
                grad_group,
                preferred_element_type=jnp.float32,
            )
            query_acc = lax.dynamic_update_index_in_dim(query_acc, grad_query, index, 2)
            key_acc = lax.dynamic_update_slice_in_dim(key_acc, grad_key, index * head_dim, 2)
            value_acc = lax.dynamic_update_slice_in_dim(value_acc, grad_value, index * head_dim, 2)
            return (query_acc, key_acc, value_acc)

        query_acc, key_acc, value_acc = lax.fori_loop(
            0,
            kv_heads,
            backward_head,
            (
                jnp.zeros((seqs, span, kv_heads, group, head_dim), jnp.float32),
                jnp.zeros((seqs, length, kv_width), jnp.float32),
                jnp.zeros((seqs, length, kv_width), jnp.float32),
            ),
        )
        key_back, value_back = (
            lax.psum_scatter(
                acc.astype(jnp.bfloat16), "ctx", scatter_dimension=1, tiled=True
            ).astype(jnp.float32)
            for acc in (key_acc, value_acc)
        )
        query_rot = rotate_back(
            query_acc.reshape(seqs, span, heads, head_dim), self.cosine, self.sine
        )
        query_back, query_gain_terms = norm_back(query_rot, self.query_heads, self.gain_query)
        key_rot = rotate_back(
            key_back.reshape(seqs, span, kv_heads, head_dim), self.cosine, self.sine
        )
        key_grad, key_gain_terms = norm_back(key_rot, self.key_heads, self.gain_key)
        lows = (
            query_back.reshape(rows, heads * head_dim).astype(jnp.bfloat16),
            key_grad.reshape(rows, kv_width).astype(jnp.bfloat16),
            value_back.reshape(rows, kv_width).astype(jnp.bfloat16),
        )
        normed_grad = sum(product_back(g, w) for g, w in zip(lows, self.weights))
        self.grads = tuple(
            rep_sum(
                lax.psum_scatter(
                    product_rows(self.normed, g).astype(jnp.bfloat16),
                    "ctx",
                    scatter_dimension=0,
                    tiled=True,
                )
            )
            for g in lows
        )
        gain_terms = (
            jnp.sum(query_gain_terms, axis=(0, 1, 2)),
            jnp.sum(key_gain_terms, axis=(0, 1, 2)),
        )
        self.normed_grad, self.gain_terms = normed_grad, gain_terms

    def finish(self, grad_resid, ffn_terms):
        back_one, attn_terms = norm_back(self.normed_grad, self.tokens, self.gain_attn)
        query_gain, key_gain = self.gain_terms
        column_one = jnp.concatenate([jnp.sum(attn_terms, axis=0), query_gain])
        column_two = jnp.concatenate([ffn_terms, key_gain])
        grads = self.weight_grads(jnp.stack([column_one, column_two], axis=1))
        return grad_resid + back_one, self.resid + self.added.astype(jnp.float32), grads

    def weight_grads(self, gains_term):
        parts = self.dims[0]
        reps = lax.axis_size("rep")
        shard = self.dims[3] // parts
        out = swap(rep_scatter(owner_blocks(self.out_term, parts, reps)))
        out = jnp.sum(out.astype(jnp.float32), axis=0).astype(jnp.bfloat16)
        gate, up, down = self.feed_terms
        gate, up = (
            rep_gather(columns_joined(swap(rep_scatter(owner_blocks(term, parts, reps)))))
            for term in (gate, up)
        )
        down = rep_gather(rep_scatter(down.reshape(reps, -1, down.shape[1])))
        gains = rep_sum(lax.psum_scatter(gains_term, "ctx", scatter_dimension=0, tiled=True))
        return self.grads + (
            rep_gather(out).reshape(shard, -1),
            gate.reshape(shard, -1),
            up.reshape(shard, -1),
            down.reshape(-1, down.shape[2]),
            gains,
        )


def feed_plain(normed, grad_all, w_gate, w_up, w_down):
    low = jnp.bfloat16
    rows, width = normed.shape
    parts = lax.axis_size("ctx")
    normed_all = gather(normed).reshape(parts * rows, width)
    grad_all = grad_all.reshape(parts * rows, width)
    gate = product(normed_all, w_gate)
    up = product(normed_all, w_up)
    sigma = jax.nn.sigmoid(gate)
    hidden_low = (gate * sigma * up).astype(low)
    added = scatter_sum(product(hidden_low, w_down).astype(low).reshape(parts, rows, width))
    grad_hidden = product_back(grad_all, w_down)
    up_grad_low = (grad_hidden * gate * sigma).astype(low)
    gate_grad_low = (grad_hidden * up * sigma * (1.0 + gate * (1.0 - sigma))).astype(low)
    back = product_back(gate_grad_low, w_gate) + product_back(up_grad_low, w_up)
    return (
        added,
        scatter_sum(back.astype(low).reshape(parts, rows, width)),
        product_rows(normed_all, gate_grad_low),
        product_rows(normed_all, up_grad_low),
        product_rows(hidden_low, grad_all),
    )


def owner_blocks(term, parts, reps):
    rows, cols = term.shape
    return term.reshape(parts, reps, rows // (parts * reps), cols).transpose(1, 0, 2, 3)


def body(

    tokens,
    cotangent,
    query_weight,
    key_weight,
    value_weight,
    output_weight,
    gate_weight,
    up_weight,
    down_weight,
    norm_gains,
    first_query,
    first_key,
    first_value,
    first_output,
    first_gate,
    first_up,
    first_down,
    first_gains,
    second_query,
    second_key,
    second_value,
    second_output,
    second_gate,
    second_up,
    second_down,
    second_gains,
):
    seqs, span, width = tokens.shape
    rows = seqs * span
    head_dim = HD
    heads = query_weight.shape[1] // head_dim
    kv_heads = key_weight.shape[1] // head_dim
    parts = lax.axis_size("ctx")
    dims = (parts, seqs, span, width, head_dim, heads, kv_heads)
    low = jnp.bfloat16
    reps = lax.axis_size("rep")
    packs = parts == kv_heads and reps == 4 and seqs * head_dim == 128
    packs = packs and feed_fits(parts, rows, width, down_weight.shape[0])
    attention = (HeadAttention if packs else RowAttention)(
        dims,
        (query_weight, key_weight, value_weight, output_weight),
        (gate_weight, up_weight),
        down_weight,
        norm_gains,
        tokens,
        cotangent,
    )
    grad_low = cotangent.reshape(rows, width)
    grad_resid, ffn_terms = attention.backward(attention.feed(), grad_low)
    weights = (
        query_weight,
        key_weight,
        value_weight,
        output_weight,
        gate_weight,
        up_weight,
        down_weight,
        norm_gains,
    )
    firsts = (
        first_query,
        first_key,
        first_value,
        first_output,
        first_gate,
        first_up,
        first_down,
        first_gains,
    )
    seconds = (
        second_query,
        second_key,
        second_value,
        second_output,
        second_gate,
        second_up,
        second_down,
        second_gains,
    )
    rates = (0.05, 0.05, 0.05, 0.3, 0.05, 0.05, 0.05, 0.5)
    decays = (0.1, 0.1, 0.1, 0.1, 0.1, 0.1, 0.1, 0.0)
    input_gradient, activations, grads = attention.finish(grad_resid, ffn_terms)
    activations = activations.astype(low).reshape(seqs, span, width)
    input_gradient = input_gradient.reshape(seqs, span, width)
    updated = [
        adamw(w, g.astype(jnp.float32), m, u, rate, decay)
        for w, g, m, u, rate, decay in zip(weights, grads, firsts, seconds, rates, decays)
    ]
    return (
        activations,
        input_gradient,
        updated[0][0],
        updated[1][0],
        updated[2][0],
        updated[3][0],
        updated[4][0],
        updated[5][0],
        updated[6][0],
        updated[7][0],
        updated[0][1],
        updated[1][1],
        updated[2][1],
        updated[3][1],
        updated[4][1],
        updated[5][1],
        updated[6][1],
        updated[7][1],
        updated[0][2],
        updated[1][2],
        updated[2][2],
        updated[3][2],
        updated[4][2],
        updated[5][2],
        updated[6][2],
        updated[7][2],
    )


def solution(mesh):
    placed = (
        P("rep", "ctx", None),
        P("rep", "ctx", None),
        P("ctx", None),
        P("ctx", None),
        P("ctx", None),
        P("ctx", None),
        P("ctx", None),
        P("ctx", None),
        P("ctx", None),
        P("ctx", None),
        P("ctx", None),
        P("ctx", None),
        P("ctx", None),
        P("ctx", None),
        P("ctx", None),
        P("ctx", None),
        P("ctx", None),
        P("ctx", None),
        P("ctx", None),
        P("ctx", None),
        P("ctx", None),
        P("ctx", None),
        P("ctx", None),
        P("ctx", None),
        P("ctx", None),
        P("ctx", None),
    )
    return jax.shard_map(
        body,
        mesh=mesh,
        in_specs=placed,
        out_specs=(
            P("rep", "ctx", None),
            P("rep", "ctx", None),
            P("ctx", None),
            P("ctx", None),
            P("ctx", None),
            P("ctx", None),
            P("ctx", None),
            P("ctx", None),
            P("ctx", None),
            P("ctx", None),
            P("ctx", None),
            P("ctx", None),
            P("ctx", None),
            P("ctx", None),
            P("ctx", None),
            P("ctx", None),
            P("ctx", None),
            P("ctx", None),
            P("ctx", None),
            P("ctx", None),
            P("ctx", None),
            P("ctx", None),
            P("ctx", None),
            P("ctx", None),
            P("ctx", None),
            P("ctx", None),
        ),
        check_vma=False,
    )
```
